32 devices in a mesh: loop: 16 (over z, y, x), grp: 2 (over core).
Axes of the slice: x: 2, y: 2, z: 4, core: 2. Of those that a mesh axis runs over, the one named last changes fastest.
Arguments:
- particles: bfloat16 [2048, 3456], P('loop'), may hold values from -32 to 32
- references: bfloat16 [64, 3456], P(('loop', 'grp')), may hold values from -6 to 6
- classes: int32 [2048], P(('loop', 'grp')), may hold values from 0 to 63, as said below
- angles: int32 [2048], P(('loop', 'grp')), may hold values from 0 to 71
- weights: int32 [2048], P(('loop', 'grp')), may hold values from 1 to 4
Outputs:
- log_evidence: float32 [2048], P(('loop', 'grp'))
- class_average: float32 [64, 3456], P(('loop', 'grp'))
The draws below stay inside these ranges and needn't reach their ends.
Inputs may be any that keep to these rules, and one draw needn't show every extreme that they name: Call the classes c with the same value of c // 4 the classes of one owner. In each aligned block of 64 rows at most 8 particles name the classes of one owner, and one owner receives exactly 8 from every block. Every class is named by some particle.
All inputs are finite; a program needn't handle non-finite values.
Results may differ from the reference program's by a relative error of at most 0.0003.
Values may be sent and summed in bfloat16 or wider, within the bound.
A program may use at most 128 MiB of HBM per device.

```python
import math
import jax
import jax.numpy as jnp
from jax import lax

RADII = 48
ANGLES = 72
CLS_DEV = 2
P_LOOP = 128
CAP = 8
CLASSES = 64
PARTICLES = 2048
N_LOOP = 16
N_GRP = 2


def planted_signs(key):
    base_key = jax.random.fold_in(key, 4242)
    signs = jnp.where(jax.random.bernoulli(base_key, 0.5, (2, RADII, ANGLES)), 1.0, -1.0).astype(jnp.float32)
    lower_mask = (jnp.arange(RADII) < RADII // 2).astype(jnp.float32)[:, None]
    return (signs[0] * lower_mask, signs[1] * (1.0 - lower_mask))


def draw_references(key, part):
    flat_len = RADII * ANGLES
    values = jnp.clip(jax.random.normal(jax.random.fold_in(key, 32), (CLASSES, flat_len), jnp.float32), -6.0, 6.0)
    lower_cycle, upper_cycle = planted_signs(key)
    values = values.at[0].set(lower_cycle.reshape(-1)).at[1].set(upper_cycle.reshape(-1))
    return values.astype(jnp.bfloat16)


def plant_rows(key, values, row_count, flat_len):
    planted = jax.random.randint(jax.random.fold_in(key, 23), (row_count,), 0, 32) == 0
    target = 150.0 + 50.0 * jax.random.randint(jax.random.fold_in(key, 24), (row_count,), 0, 4).astype(jnp.float32)
    spacing = jax.random.uniform(jax.random.fold_in(key, 25), (row_count,), jnp.float32, 1.0, 3.0)
    per_unit = 2.0 / math.sqrt(flat_len) * (RADII // 2) * ANGLES
    lower_cycle, upper_cycle = planted_signs(key)
    angle_grid = jnp.arange(ANGLES, dtype=jnp.int32)
    first_turn = jax.random.randint(jax.random.fold_in(key, 26), (row_count, 1), 0, ANGLES)
    second_turn = jax.random.randint(jax.random.fold_in(key, 27), (row_count, 1), 0, ANGLES)
    lower_rolled = jnp.take(lower_cycle, (angle_grid[None, :] + first_turn) % ANGLES, axis=1)
    upper_rolled = jnp.take(upper_cycle, (angle_grid[None, :] + second_turn) % ANGLES, axis=1)
    mixed = (target / per_unit)[None, :, None] * lower_rolled + ((target - spacing) / per_unit)[None, :, None] * upper_rolled
    mixed = jnp.transpose(mixed, (1, 0, 2)).reshape(row_count, flat_len)
    return jnp.where(planted[:, None], mixed, values)


def draw_particles(key, part):
    row_count = P_LOOP * N_LOOP
    flat_len = RADII * ANGLES
    values = jnp.clip(jax.random.normal(jax.random.fold_in(key, 28), (row_count, flat_len), jnp.float32), -6.0, 6.0)
    values = plant_rows(key, values, row_count, flat_len)
    return values.astype(jnp.bfloat16)


def draw_classes(key, part):
    half_rows = P_LOOP // 2
    owner_count = N_LOOP
    per_owner = CLS_DEV * N_GRP
    slot_count = owner_count * CAP
    ranking = jax.random.permutation(jax.random.fold_in(key, 11), owner_count)
    busiest = jnp.argmin(ranking)
    offset = jax.random.randint(jax.random.fold_in(key, 12), (), 0, owner_count)
    slot_index = jnp.arange(slot_count, dtype=jnp.int32)
    owner_of = slot_index // CAP
    lane_of = slot_index % CAP

    def one_block(block_index):
        block_key = jax.random.fold_in(key, 1000 + block_index)
        jitter = jax.random.randint(jax.random.fold_in(block_key, 1), (slot_count,), 0, 512)
        priority = 1024 + jitter + ranking[owner_of] * 512 // owner_count
        priority = jnp.where(owner_of == busiest, lane_of, priority)
        position = block_index % owner_count
        half_index = block_index // owner_count
        forced_member = jnp.zeros((slot_count,), jnp.int32) - 1
        for member in range(CLS_DEV):
            target_owner = (position + member + offset) % owner_count
            marked = (owner_of == target_owner) & (lane_of == 0)
            priority = jnp.where(marked, CAP + member, priority)
            forced_member = jnp.where(marked, half_index * CLS_DEV + member, forced_member)
        ordering = jnp.argsort(priority * slot_count + slot_index)
        chosen = ordering[:half_rows]
        random_member = jax.random.randint(jax.random.fold_in(block_key, 2), (half_rows,), 0, per_owner)
        picked_forced = forced_member[chosen]
        member_of = jnp.where(picked_forced >= 0, picked_forced, random_member)
        picked = owner_of[chosen] * per_owner + member_of
        shuffle = jax.random.permutation(jax.random.fold_in(block_key, 3), half_rows)
        return picked[shuffle]
    blocks = jax.vmap(one_block)(jnp.arange(N_LOOP * N_GRP, dtype=jnp.int32))
    return blocks.reshape(-1).astype(jnp.int32)


def set_ends(array, own_key, low, high):
    place = [jax.random.randint(jax.random.fold_in(own_key, axis), (), 0, length) for axis, length in enumerate(array.shape)]
    longest = array.shape.index(max(array.shape))
    neighbour = place[:longest] + [(place[longest] + 1) % array.shape[longest]] + place[longest + 1:]
    return array.at[tuple(place)].set(low).at[tuple(neighbour)].set(high)


def setup_inputs(seed: int = 0) -> dict:
    splits = jax.random.split(jax.random.key(seed), 6)
    particles = draw_particles(jax.random.fold_in(splits[5], 71), 0)
    references = draw_references(jax.random.fold_in(splits[5], 71), 0)
    classes = draw_classes(jax.random.fold_in(splits[5], 71), 0)
    angles = set_ends(jax.random.randint(splits[3], (PARTICLES,), 0, ANGLES), jax.random.fold_in(splits[3], 1), 0, ANGLES - 1).astype(jnp.int32)
    weights = set_ends(jax.random.randint(splits[4], (PARTICLES,), 1, 5), jax.random.fold_in(splits[4], 1), 1, 4).astype(jnp.int32)
    return {"particles": particles, "references": references, "classes": classes, "angles": angles, "weights": weights}


score_factor = 2.0

def turned_rows(ref_block, radius_count, angle_count):
    block_rows = ref_block.shape[0]
    polar_rows = ref_block.reshape(block_rows, radius_count, angle_count)
    angle_grid = jnp.arange(angle_count, dtype=jnp.int32)
    source_index = ((angle_grid[:, None] + angle_grid[None, :]) % angle_count).astype(jnp.int32)
    rotated = jnp.take(polar_rows, source_index, axis=2)
    rotated = jnp.transpose(rotated, (0, 2, 1, 3))
    return rotated.reshape(block_rows * angle_count, radius_count * angle_count)

def reference(particles, references, classes, angles, weights):
    flat_len = RADII * ANGLES
    score_scale = score_factor / math.sqrt(flat_len)
    group_size = CLS_DEV * N_GRP
    ref_groups = references.reshape(CLASSES // group_size, group_size, flat_len)
    row_count = particles.shape[0]

    def advance(running, ref_block):
        highest, summed = running
        rotated = turned_rows(ref_block, RADII, ANGLES)
        scores = lax.dot_general(particles, rotated, (((1,), (1,)), ((), ())), preferred_element_type=jnp.float32) * score_scale
        new_max = jnp.maximum(highest, lax.optimization_barrier(jnp.max(scores, axis=1)))
        summed = summed * jnp.exp(highest - new_max) + lax.optimization_barrier(jnp.sum(jnp.exp(scores - new_max[:, None]), axis=1))
        return ((new_max, summed), None)
    starting = (jnp.full((row_count,), -jnp.inf, jnp.float32), jnp.zeros((row_count,), jnp.float32))
    (highest, summed), _ = lax.scan(advance, starting, ref_groups)
    log_evidence = highest + jnp.log(summed)
    polar_rows = particles.reshape(row_count, RADII, ANGLES).astype(jnp.float32)
    source_angle = (jnp.arange(ANGLES, dtype=jnp.int32)[None, :] - angles[:, None]) % ANGLES
    aligned = jnp.take_along_axis(polar_rows, source_angle.astype(jnp.int32)[:, None, :], axis=2).reshape(row_count, flat_len)
    weighted = (jnp.arange(CLASSES, dtype=jnp.int32)[:, None] == classes[None, :]).astype(jnp.float32) * weights.astype(jnp.float32)[None, :]
    class_sums = jnp.dot(weighted, aligned, precision=lax.Precision.HIGHEST, preferred_element_type=jnp.float32)
    class_weight = lax.optimization_barrier(jnp.sum(weighted, axis=1))
    class_average = class_sums / class_weight[:, None]
    return (log_evidence, class_average)
```

```python
import functools
import math

import jax
import jax.numpy as jnp
from jax import lax
from jax.experimental import pallas as pl
from jax.experimental.pallas import tpu as pltpu
from jax.sharding import PartitionSpec as P

RADII = 48
ANGLES = 72
FLAT = RADII * ANGLES
LANES = 128
TILES = FLAT // LANES
WIRE = 32
STEP = 8
TURNS = ANGLES // STEP
EXT = STEP - 2
SCALE = 2.0 / math.sqrt(FLAT)
MESH = pl.DeviceIdType.MESH


def kernel(
    n, cls_dev,
    x_ref, ref_ref, cls_ref, ang_ref, wgt_ref,
    logev_ref, avg_ref,
    wire, wide, rbig, lab, stat, flat_t, ping, pong, alig, ptx, part, got,
    r_send, r_recv, s_send, s_recv, c_send, c_recv,
):
    me = lax.axis_index("loop")
    grp = lax.axis_index("grp")
    other = 1 - grp
    rows = x_ref.shape[0]
    half = rows // 2
    cls_count = n * cls_dev

    def peer(k):
        return {"loop": lax.rem(me + k, n)}

    def ref_copy(k):
        return pltpu.make_async_remote_copy(
            src_ref=wire.at[0], dst_ref=wire.at[k], send_sem=r_send.at[k], recv_sem=r_recv.at[k],
            device_id=peer(k), device_id_type=MESH)

    def sum_copy(k):
        return pltpu.make_async_remote_copy(
            src_ref=part.at[lax.rem(me + k, n)], dst_ref=got.at[k], send_sem=s_send.at[k],
            recv_sem=s_recv.at[k], device_id=peer(k), device_id_type=MESH)

    def core_copy(buf, k):
        return pltpu.make_async_remote_copy(
            src_ref=buf.at[0], dst_ref=buf.at[1], send_sem=c_send.at[k], recv_sem=c_recv.at[k],
            device_id={"grp": other}, device_id_type=MESH)

    barrier = pltpu.get_barrier_semaphore()

    @pl.loop(1, n)
    def _(k):
        pl.semaphore_signal(barrier, inc=1, device_id=peer(k), device_id_type=MESH)

    pl.semaphore_signal(barrier, inc=1, device_id={"grp": other}, device_id_type=MESH)

    wire[0] = ref_ref[...]
    lane = lax.broadcasted_iota(jnp.int32, (1, rows), 1)
    mine = (lane // half) == grp
    for i, src in enumerate((cls_ref, ang_ref, wgt_ref)):
        both = jnp.concatenate([src[...], src[...]], axis=1)
        lab[0, i:i + 1, :] = jnp.where(mine, both, 0)

    pl.semaphore_wait(barrier, n)

    label_copy = core_copy(lab, 0)
    label_copy.start()

    @pl.loop(1, n)
    def _(k):
        ref_copy(k).start()

    for i in range(TILES):
        tile = x_ref[:, i * LANES:(i + 1) * LANES].astype(jnp.float32)
        flat_t[i * LANES:(i + 1) * LANES, :] = tile.T

    for t in range(ANGLES):
        rad = flat_t[pl.ds(t, RADII, stride=ANGLES), :]
        ping[t] = rad
        low = rad.astype(jnp.bfloat16)
        for shift in range(2):
            for at in (t + shift + EXT, t + shift + EXT - ANGLES):
                if 0 <= at < ANGLES + EXT:
                    ptx[at * RADII:(at + 1) * RADII, shift * rows:(shift + 1) * rows] = low

    label_copy.wait()
    labels = lab[0, 0:8, :] + lab[1, 0:8, :]
    classes, angles, weights = labels[0:1], labels[1:2], labels[2:3]

    src, dst = ping, pong
    for bit in range(7):
        on = jnp.broadcast_to(((angles >> bit) & 1) == 1, (8, rows))
        by = 1 << bit

        def turn(t, _, src=src, dst=dst, on=on, by=by):
            back = lax.rem(t + (ANGLES - by), ANGLES)
            for j in range(RADII // 8):
                rs = slice(j * 8, (j + 1) * 8)
                dst[t, rs, :] = jnp.where(on, src[back, rs, :], src[t, rs, :])
            return 0

        lax.fori_loop(0, ANGLES, turn, 0, unroll=4)
        src, dst = dst, src

    for t in range(ANGLES):
        flat_t[pl.ds(t, RADII, stride=ANGLES), :] = src[t]
    alig[0:FLAT, :] = flat_t[...].astype(jnp.bfloat16)
    alig[FLAT:, :] = jnp.ones((LANES, rows), jnp.bfloat16)

    row = lax.broadcasted_iota(jnp.int32, (cls_count, rows), 0)
    named = (row // cls_dev) * (2 * cls_dev) + grp * cls_dev + row % cls_dev
    pick = jnp.where(named == classes, weights, 0).astype(jnp.float32).astype(jnp.bfloat16)
    chunk = 512
    for i in range((FLAT + LANES) // chunk):
        sl = slice(i * chunk, (i + 1) * chunk)
        sums = lax.dot_general(pick, alig[sl, :], (((1,), (1,)), ((), ())),
                               preferred_element_type=jnp.float32)
        for o in range(n):
            part[o, :, sl] = sums[o * cls_dev:(o + 1) * cls_dev, :]

    @pl.loop(1, n)
    def _(k):
        sum_copy(k).start()

    @pl.loop(1, n)
    def _(k):
        ref_copy(k).wait()

    wide[...] = wire[...].reshape(n * cls_dev * WIRE, LANES).astype(jnp.float32)
    for i in range(TILES):
        tile = wide[pl.ds(i, cls_count, stride=WIRE), :].astype(jnp.bfloat16)
        for s1 in range(TURNS):
            at = (i - 3 * s1) % TILES
            rbig[s1 * cls_count:(s1 + 1) * cls_count, at * LANES:(at + 1) * LANES] = tile

    tops, mass = [], []
    for q in range(STEP // 2):
        at = (EXT - 2 * q) * RADII
        score = jnp.dot(rbig[...], ptx[at:at + FLAT, :], preferred_element_type=jnp.float32) * SCALE
        top = jnp.max(score, axis=0, keepdims=True)
        total = jnp.sum(jnp.exp(score - top), axis=0, keepdims=True)
        for h in range(2):
            tops.append(top[:, h * rows:(h + 1) * rows])
            mass.append(total[:, h * rows:(h + 1) * rows])
    top = functools.reduce(jnp.maximum, tops)
    total = functools.reduce(jnp.add, [m * jnp.exp(t - top) for t, m in zip(tops, mass)])
    stat[0, 0:1, :] = top
    stat[0, 1:2, :] = total
    stat_copy = core_copy(stat, 1)
    stat_copy.start()

    @pl.loop(1, n)
    def _(k):
        sum_copy(k).wait()

    acc = part[me]
    for k in range(1, n):
        acc = acc + got[k]
    avg_ref[...] = acc[:, :FLAT] / acc[:, FLAT:FLAT + 1]

    stat_copy.wait()
    top2, total2 = stat[1, 0:1, :], stat[1, 1:2, :]
    high = jnp.maximum(top, top2)
    out = high + jnp.log(total * jnp.exp(top - high) + total2 * jnp.exp(top2 - high))
    logev_ref[...] = jnp.where(grp == 0, out[:, :half], out[:, half:])


def local(particles, references, classes, angles, weights):
    rows = particles.shape[0]
    half = rows // 2
    cls_dev = references.shape[0]
    n = lax.axis_size("loop")
    cls_count = n * cls_dev
    polar = references.reshape(cls_dev, RADII, ANGLES).transpose(0, 2, 1).reshape(cls_dev, TILES, LANES)
    polar = jnp.pad(polar, ((0, 0), (0, WIRE - TILES), (0, 0))).reshape(cls_dev * WIRE, LANES)
    vmem = pl.BlockSpec(memory_space=pltpu.VMEM)
    f32, bf16 = jnp.float32, jnp.bfloat16
    logev, avg = pl.pallas_call(
        functools.partial(kernel, n, cls_dev),
        out_shape=(
            jax.ShapeDtypeStruct((1, half), f32),
            jax.ShapeDtypeStruct((cls_dev, FLAT), f32),
        ),
        in_specs=[vmem] * 5,
        out_specs=(vmem, vmem),
        scratch_shapes=[
            pltpu.VMEM((n, cls_dev * WIRE, LANES), bf16),
            pltpu.VMEM((n * cls_dev * WIRE, LANES), f32),
            pltpu.VMEM((TURNS * cls_count, FLAT), bf16),
            pltpu.VMEM((2, 8, rows), jnp.int32),
            pltpu.VMEM((2, 8, rows), f32),
            pltpu.VMEM((FLAT, rows), f32),
            pltpu.VMEM((ANGLES, RADII, rows), f32),
            pltpu.VMEM((ANGLES, RADII, rows), f32),
            pltpu.VMEM((FLAT + LANES, rows), bf16),
            pltpu.VMEM(((ANGLES + EXT) * RADII, 2 * rows), bf16),
            pltpu.VMEM((n, cls_dev, FLAT + LANES), f32),
            pltpu.VMEM((n, cls_dev, FLAT + LANES), f32),
            pltpu.SemaphoreType.DMA((n,)),
            pltpu.SemaphoreType.DMA((n,)),
            pltpu.SemaphoreType.DMA((n,)),
            pltpu.SemaphoreType.DMA((n,)),
            pltpu.SemaphoreType.DMA((2,)),
            pltpu.SemaphoreType.DMA((2,)),
        ],
        compiler_params=pltpu.CompilerParams(
            collective_id=0, has_side_effects=True, vmem_limit_bytes=56 * 1024 * 1024),
    )(particles, polar, classes.reshape(1, half), angles.reshape(1, half), weights.reshape(1, half))
    return logev.reshape(half), avg


def solution(mesh):
    return jax.shard_map(
        local,
        mesh=mesh,
        in_specs=(
            P("loop", None),
            P(("loop", "grp"), None),
            P(("loop", "grp")),
            P(("loop", "grp")),
            P(("loop", "grp")),
        ),
        out_specs=(P(("loop", "grp")), P(("loop", "grp"), None)),
        check_vma=False,
    )
```

```python
import functools
import math

import jax
import jax.numpy as jnp
from jax import lax
from jax.experimental import pallas as pl
from jax.experimental.pallas import tpu as pltpu
from jax.sharding import PartitionSpec as P

RADII = 48
ANGLES = 72
FLAT = RADII * ANGLES
LANES = 128
TILES = FLAT // LANES
WIRE = 32
STEP = 8
TURNS = ANGLES // STEP
EXT = STEP - 2
CHUNKS = 3
CHUNK_R = RADII // CHUNKS
CHUNK = FLAT // CHUNKS
WINDOW = 24
INNER = 4
SCALE = 2.0 / math.sqrt(FLAT)
MESH = pl.DeviceIdType.MESH


def chunk_lanes(g):
    return CHUNK + (LANES if g == 0 else 0)


def kernel(
    ni, no, cls_dev,
    x_ref, ref_ref, cls_ref, ang_ref, wgt_ref,
    out_ref,
    square, turned, wide, wire, rbig, lab, stat, flat_t, ping, flat_a, ptx,
    part0, part1, part2, gota0, gota1, gota2, sum0, sum1, sum2, gotb0, gotb1, gotb2,
    z_send, z_recv, i_send, i_recv, f_send, f_recv, a_send, a_recv, b_send, b_recv, c_send, c_recv,
):
    part, gota = (part0, part1, part2), (gota0, gota1, gota2)
    sums, gotb = (sum0, sum1, sum2), (gotb0, gotb1, gotb2)
    me = lax.axis_index("loop")
    grp = lax.axis_index("grp")
    outer, inner = me // ni, lax.rem(me, ni)
    rows = x_ref.shape[0]
    half = rows // 2
    cls_count = ni * no * cls_dev

    def outer_peer(k):
        return {"loop": lax.rem(outer + k, no) * ni + inner}

    def inner_peer(k):
        return {"loop": outer * ni + lax.rem(inner + k, ni)}

    other = {"grp": 1 - grp}

    def remote(src, dst, send, recv, to):
        return pltpu.make_async_remote_copy(
            src_ref=src, dst_ref=dst, send_sem=send, recv_sem=recv, device_id=to, device_id_type=MESH)

    def z_copy(k):
        return remote(wire.at[0, 0], wire.at[0, k], z_send.at[k], z_recv.at[k], outer_peer(k))

    def i_copy(k):
        return remote(wire.at[0, 0], wire.at[k, 0], i_send.at[k], i_recv.at[k], inner_peer(k))

    def f_copy(k):
        return remote(wire.at[0, 1:], wire.at[k, 1:], f_send.at[k], f_recv.at[k], inner_peer(k))

    def a_copy(g, k):
        return remote(part[g].at[lax.rem(inner + k, ni)], gota[g].at[k],
                      a_send.at[g, k], a_recv.at[g, k], inner_peer(k))

    def b_copy(g, k):
        return remote(sums[g].at[lax.rem(outer + k, no)], gotb[g].at[k],
                      b_send.at[g, k], b_recv.at[g, k], outer_peer(k))

    def core_copy(buf, k):
        return remote(buf.at[0], buf.at[1], c_send.at[k], c_recv.at[k], other)

    barrier = pltpu.get_barrier_semaphore()

    @pl.loop(1, no)
    def _(k):
        pl.semaphore_signal(barrier, inc=1, device_id=outer_peer(k), device_id_type=MESH)

    for k in range(1, ni):
        pl.semaphore_signal(barrier, inc=1, device_id=inner_peer(k), device_id_type=MESH)
    pl.semaphore_signal(barrier, inc=1, device_id=other, device_id_type=MESH)

    lane = lax.broadcasted_iota(jnp.int32, (1, rows), 1)
    mine = (lane // half) == grp
    lab[0] = jnp.zeros((8, rows), jnp.int32)
    for i, src in enumerate((cls_ref, ang_ref, wgt_ref)):
        both = jnp.concatenate([src[...], src[...]], axis=1)
        lab[0, i:i + 1, :] = jnp.where(mine, both, 0)

    refs = ref_ref[...].astype(jnp.float32)
    square[...] = jnp.zeros((LANES, LANES), jnp.float32)
    wide[0:cls_dev * WIRE, :] = jnp.zeros((cls_dev * WIRE, LANES), jnp.float32)
    for c in range(cls_dev):
        for r in range(RADII):
            square[r:r + 1, 0:ANGLES] = refs[c:c + 1, r * ANGLES:(r + 1) * ANGLES]
        turned[...] = square[...].T
        line = jnp.concatenate(
            [turned[pl.ds(v, TURNS, stride=STEP), :][:, 0:RADII] for v in range(STEP)], axis=1)
        for w in range(3):
            wide[pl.ds(c * WIRE + w, TURNS, stride=3), :] = line[:, w * LANES:(w + 1) * LANES]
    wire[0, 0] = wide[0:cls_dev * WIRE, :].astype(jnp.bfloat16)

    def transpose(g):
        for i in range(g * (CHUNK // LANES), (g + 1) * (CHUNK // LANES)):
            tile = x_ref[:, i * LANES:(i + 1) * LANES].astype(jnp.float32)
            flat_t[i * LANES:(i + 1) * LANES, :] = tile.T

    transpose(0)
    pl.semaphore_wait(barrier, ni + no - 1)

    label_copy = core_copy(lab, 0)
    label_copy.start()

    @pl.loop(1, no)
    def _(k):
        z_copy(k).start()

    for k in range(1, ni):
        i_copy(k).start()

    transpose(1)
    transpose(2)

    label_copy.wait()
    labels = lab[0] + lab[1]
    classes, angles, weights = labels[0:1], labels[1:2], labels[2:3]
    bits = [jnp.broadcast_to(((angles >> b) & 1) == 1, (8, rows)) for b in range(7)]

    row = lax.broadcasted_iota(jnp.int32, (cls_count, rows), 0)
    owner = row // cls_dev
    named = (((owner % no) * ni + owner // no) * 2 + grp) * cls_dev + row % cls_dev
    pick = jnp.where(named == classes, weights, 0).astype(jnp.float32).astype(jnp.bfloat16)

    def chunk_sums(g):
        for r in range(g * CHUNK_R, (g + 1) * CHUNK_R, 8):
            base = r * ANGLES
            for t0 in range(0, ANGLES, WINDOW):
                vals = {t: flat_t[pl.ds(base + t % ANGLES, 8, stride=ANGLES), :]
                        for t in range(t0 - 7, t0 + WINDOW)}
                for b in range(3):
                    low = t0 - 7 + (2 << b) - 1
                    vals = {t: jnp.where(bits[b], vals[t - (1 << b)], vals[t])
                            for t in range(low, t0 + WINDOW)}
                for t in range(t0, t0 + WINDOW):
                    ping[t] = vals[t]
            for v in range(STEP):
                vals = [ping[STEP * u + v] for u in range(TURNS)]
                for b in range(4):
                    vals = [jnp.where(bits[3 + b], vals[(u - (1 << b)) % TURNS], vals[u])
                            for u in range(TURNS)]
                for u in range(TURNS):
                    flat_a[pl.ds(base + STEP * u + v, 8, stride=ANGLES), :] = vals[u]
        aligned = flat_a[g * CHUNK:(g + 1) * CHUNK, :].astype(jnp.bfloat16)
        if g == 0:
            aligned = jnp.concatenate([aligned, jnp.ones((LANES, rows), jnp.bfloat16)], axis=0)
        mine_sums = lax.dot_general(pick, aligned, (((1,), (1,)), ((), ())),
                                    preferred_element_type=jnp.float32)
        for o in range(ni * no):
            part[g][o // no, o % no] = mine_sums[o * cls_dev:(o + 1) * cls_dev, :]
        for k in range(1, ni):
            a_copy(g, k).start()

    chunk_sums(0)

    @pl.loop(1, no)
    def _(k):
        z_copy(k).wait()

    for k in range(1, ni):
        f_copy(k).start()

    for g in range(1, CHUNKS):
        chunk_sums(g)

    for t in range(ANGLES):
        low = flat_t[pl.ds(t, RADII, stride=ANGLES), :].astype(jnp.bfloat16)
        for shift in range(2):
            for at in (t + shift + EXT, t + shift + EXT - ANGLES):
                if 0 <= at < ANGLES + EXT:
                    ptx[at * RADII:(at + 1) * RADII, shift * rows:(shift + 1) * rows] = low

    def second(g):
        for k in range(1, ni):
            a_copy(g, k).wait()
        acc = part[g][inner]
        for k in range(1, ni):
            acc = acc + gota[g][k]
        sums[g][...] = acc

        @pl.loop(1, no)
        def _(k):
            b_copy(g, k).start()

    second(0)

    for k in range(1, ni):
        i_copy(k).wait()
        f_copy(k).wait()

    wide[...] = wire[...].reshape(cls_count * WIRE, LANES).astype(jnp.float32)
    for i in range(TILES):
        tile = wide[pl.ds(i, cls_count, stride=WIRE), :].astype(jnp.bfloat16)
        for s1 in range(TURNS):
            at = (i - 3 * s1) % TILES
            rbig[s1 * cls_count:(s1 + 1) * cls_count, at * LANES:(at + 1) * LANES] = tile

    tops, mass = [], []
    for q in range(STEP // 2):
        at = (EXT - 2 * q) * RADII
        score = jnp.dot(rbig[...], ptx[at:at + FLAT, :], preferred_element_type=jnp.float32) * SCALE
        top = jnp.max(score, axis=0, keepdims=True)
        total = jnp.sum(jnp.exp(score - top), axis=0, keepdims=True)
        for h in range(2):
            tops.append(top[:, h * rows:(h + 1) * rows])
            mass.append(total[:, h * rows:(h + 1) * rows])
        if q + 1 < CHUNKS:
            second(q + 1)
    top = functools.reduce(jnp.maximum, tops)
    total = functools.reduce(jnp.add, [m * jnp.exp(t - top) for t, m in zip(tops, mass)])
    stat[0] = jnp.concatenate([top, total, jnp.zeros((6, rows), jnp.float32)], axis=0)
    stat_copy = core_copy(stat, 1)
    stat_copy.start()

    weight = None
    for g in range(CHUNKS):
        @pl.loop(1, no)
        def _(k):
            b_copy(g, k).wait()

        acc = sums[g][outer]
        for k in range(1, no):
            acc = acc + gotb[g][k]
        if weight is None:
            weight = acc[:, CHUNK:CHUNK + 1]
        out_ref[:, g * CHUNK:(g + 1) * CHUNK] = acc[:, :CHUNK] / weight

    stat_copy.wait()
    top2, total2 = stat[1, 0:1, :], stat[1, 1:2, :]
    high = jnp.maximum(top, top2)
    out = high + jnp.log(total * jnp.exp(top - high) + total2 * jnp.exp(top2 - high))
    out = jnp.where(grp == 0, out, jnp.concatenate([out[:, half:], out[:, :half]], axis=1))
    out_ref[:, FLAT:] = jnp.broadcast_to(out, (cls_dev, rows))


def local(particles, references, classes, angles, weights):
    rows = particles.shape[0]
    half = rows // 2
    cls_dev = references.shape[0]
    n = lax.axis_size("loop")
    ni = INNER
    no = n // ni
    cls_count = n * cls_dev
    vmem = pl.BlockSpec(memory_space=pltpu.VMEM)
    f32, bf16 = jnp.float32, jnp.bfloat16

    def chunk_bufs(*lead):
        return [pltpu.VMEM((*lead, cls_dev, chunk_lanes(g)), f32) for g in range(CHUNKS)]

    dma = pltpu.SemaphoreType.DMA
    out = pl.pallas_call(
        functools.partial(kernel, ni, no, cls_dev),
        out_shape=jax.ShapeDtypeStruct((cls_dev, FLAT + rows), f32),
        in_specs=[vmem] * 5,
        out_specs=vmem,
        scratch_shapes=[
            pltpu.VMEM((LANES, LANES), f32),
            pltpu.VMEM((LANES, LANES), f32),
            pltpu.VMEM((cls_count * WIRE, LANES), f32),
            pltpu.VMEM((ni, no, cls_dev * WIRE, LANES), bf16),
            pltpu.VMEM((TURNS * cls_count, FLAT), bf16),
            pltpu.VMEM((2, 8, rows), jnp.int32),
            pltpu.VMEM((2, 8, rows), f32),
            pltpu.VMEM((FLAT, rows), f32),
            pltpu.VMEM((ANGLES, 8, rows), f32),
            pltpu.VMEM((FLAT, rows), f32),
            pltpu.VMEM(((ANGLES + EXT) * RADII, 2 * rows), bf16),
            *chunk_bufs(ni, no), *chunk_bufs(ni, no), *chunk_bufs(no), *chunk_bufs(no),
            dma((no,)), dma((no,)), dma((ni,)), dma((ni,)), dma((ni,)), dma((ni,)),
            dma((CHUNKS, ni)), dma((CHUNKS, ni)), dma((CHUNKS, no)), dma((CHUNKS, no)),
            dma((2,)), dma((2,)),
        ],
        compiler_params=pltpu.CompilerParams(
            collective_id=0, has_side_effects=True, vmem_limit_bytes=56 * 1024 * 1024),
    )(particles, references, classes.reshape(1, half), angles.reshape(1, half), weights.reshape(1, half))
    return out[0, FLAT:FLAT + half], out[:, :FLAT]


def solution(mesh):
    return jax.shard_map(
        local,
        mesh=mesh,
        in_specs=(
            P("loop", None),
            P(("loop", "grp"), None),
            P(("loop", "grp")),
            P(("loop", "grp")),
            P(("loop", "grp")),
        ),
        out_specs=(P(("loop", "grp")), P(("loop", "grp"), None)),
        check_vma=False,
    )
```

```python
import functools
import math

import jax
import jax.numpy as jnp
from jax import lax
from jax.experimental import pallas as pl
from jax.experimental.pallas import tpu as pltpu
from jax.sharding import PartitionSpec as P

RADII = 48
ANGLES = 72
FLAT = RADII * ANGLES
LANES = 128
TILES = FLAT // LANES
WIRE = 32
STEP = 8
TURNS = ANGLES // STEP
ODD = ANGLES + 1
EXT = STEP - 2
CHUNKS = 3
CHUNK_R = RADII // CHUNKS
CHUNK = FLAT // CHUNKS
INNER = 4
SCALE = 2.0 / math.sqrt(FLAT)
MESH = pl.DeviceIdType.MESH


def chunk_lanes(g):
    return CHUNK + (LANES if g == 0 else 0)


def kernel(
    ni, no, cls_dev,
    x_ref, ref_ref, cls_ref, ang_ref, wgt_ref,
    out_ref,
    square, turned, wide, wire, rbig, lab, stat, flat_t, padded, flat_a, ptx,
    part0, part1, part2, gota0, gota1, gota2, sum0, sum1, sum2, gotb0, gotb1, gotb2,
    z_send, z_recv, i_send, i_recv, f_send, f_recv, a_send, a_recv, b_send, b_recv, c_send, c_recv,
):
    part, gota = (part0, part1, part2), (gota0, gota1, gota2)
    sums, gotb = (sum0, sum1, sum2), (gotb0, gotb1, gotb2)
    me = lax.axis_index("loop")
    grp = lax.axis_index("grp")
    outer, inner = me // ni, lax.rem(me, ni)
    rows = x_ref.shape[0]
    half = rows // 2
    cls_count = ni * no * cls_dev

    def outer_peer(k):
        return {"loop": lax.rem(outer + k, no) * ni + inner}

    def inner_peer(k):
        return {"loop": outer * ni + lax.rem(inner + k, ni)}

    other = {"grp": 1 - grp}

    def remote(src, dst, send, recv, to):
        return pltpu.make_async_remote_copy(
            src_ref=src, dst_ref=dst, send_sem=send, recv_sem=recv, device_id=to, device_id_type=MESH)

    def z_copy(k):
        return remote(wire.at[0, 0], wire.at[0, k], z_send.at[k], z_recv.at[k], outer_peer(k))

    def i_copy(k):
        return remote(wire.at[0, 0], wire.at[k, 0], i_send.at[k], i_recv.at[k], inner_peer(k))

    def f_copy(k):
        return remote(wire.at[0, 1:], wire.at[k, 1:], f_send.at[k], f_recv.at[k], inner_peer(k))

    def a_copy(g, k):
        return remote(part[g].at[lax.rem(inner + k, ni)], gota[g].at[k],
                      a_send.at[g, k], a_recv.at[g, k], inner_peer(k))

    def b_copy(g, k):
        return remote(sums[g].at[lax.rem(outer + k, no)], gotb[g].at[k],
                      b_send.at[g, k], b_recv.at[g, k], outer_peer(k))

    def core_copy(buf, k):
        return remote(buf.at[0], buf.at[1], c_send.at[k], c_recv.at[k], other)

    barrier = pltpu.get_barrier_semaphore()

    @pl.loop(1, no)
    def _(k):
        pl.semaphore_signal(barrier, inc=1, device_id=outer_peer(k), device_id_type=MESH)

    for k in range(1, ni):
        pl.semaphore_signal(barrier, inc=1, device_id=inner_peer(k), device_id_type=MESH)
    pl.semaphore_signal(barrier, inc=1, device_id=other, device_id_type=MESH)

    lane = lax.broadcasted_iota(jnp.int32, (1, rows), 1)
    mine = (lane // half) == grp
    lab[0] = jnp.zeros((8, rows), jnp.int32)
    for i, src in enumerate((cls_ref, ang_ref, wgt_ref)):
        both = jnp.concatenate([src[...], src[...]], axis=1)
        lab[0, i:i + 1, :] = jnp.where(mine, both, 0)

    refs = ref_ref[...].astype(jnp.float32)
    square[...] = jnp.zeros((LANES, LANES), jnp.float32)
    wide[0:cls_dev * WIRE, :] = jnp.zeros((cls_dev * WIRE, LANES), jnp.float32)
    for c in range(cls_dev):
        for r in range(RADII):
            square[r:r + 1, 0:ANGLES] = refs[c:c + 1, r * ANGLES:(r + 1) * ANGLES]
        turned[...] = square[...].T
        line = jnp.concatenate(
            [turned[pl.ds(v, TURNS, stride=STEP), :][:, 0:RADII] for v in range(STEP)], axis=1)
        for w in range(3):
            wide[pl.ds(c * WIRE + w, TURNS, stride=3), :] = line[:, w * LANES:(w + 1) * LANES]
    wire[0, 0] = wide[0:cls_dev * WIRE, :].astype(jnp.bfloat16)

    def transpose(g):
        for i in range(g * (CHUNK // LANES), (g + 1) * (CHUNK // LANES)):
            tile = x_ref[:, i * LANES:(i + 1) * LANES].astype(jnp.float32)
            flat_t[i * LANES:(i + 1) * LANES, :] = tile.T

    transpose(0)
    pl.semaphore_wait(barrier, ni + no - 1)

    label_copy = core_copy(lab, 0)
    label_copy.start()

    @pl.loop(1, no)
    def _(k):
        z_copy(k).start()

    for k in range(1, ni):
        i_copy(k).start()

    transpose(1)
    transpose(2)

    label_copy.wait()
    labels = lab[0] + lab[1]
    classes, angles, weights = labels[0:1], labels[1:2], labels[2:3]
    bits = [jnp.broadcast_to(((angles >> b) & 1) == 1, (8, rows)) for b in range(7)]

    row = lax.broadcasted_iota(jnp.int32, (cls_count, rows), 0)
    owner = row // cls_dev
    named = (((owner % no) * ni + owner // no) * 2 + grp) * cls_dev + row % cls_dev
    pick = jnp.where(named == classes, weights, 0).astype(jnp.float32).astype(jnp.bfloat16)

    sub = lax.broadcasted_iota(jnp.int32, (8, rows), 0)

    def chunk_sums(g):
        for r in range(g * CHUNK_R, (g + 1) * CHUNK_R):
            base = r * ANGLES
            vals = [flat_t[base + STEP * u:base + STEP * (u + 1), :] for u in range(TURNS)]
            for b in range(4):
                vals = [jnp.where(bits[3 + b], vals[(u - (1 << b)) % TURNS], vals[u])
                        for u in range(TURNS)]
            for b in range(3):
                by = 1 << b
                moved = [pltpu.roll(v, by, 0) for v in vals]
                vals = [jnp.where(bits[b], jnp.where(sub < by, moved[(u - 1) % TURNS], moved[u]), vals[u])
                        for u in range(TURNS)]
            for u in range(TURNS):
                flat_a[base + STEP * u:base + STEP * (u + 1), :] = vals[u]
        aligned = flat_a[g * CHUNK:(g + 1) * CHUNK, :].astype(jnp.bfloat16)
        if g == 0:
            aligned = jnp.concatenate([aligned, jnp.ones((LANES, rows), jnp.bfloat16)], axis=0)
        mine_sums = lax.dot_general(pick, aligned, (((1,), (1,)), ((), ())),
                                    preferred_element_type=jnp.float32)
        for o in range(ni * no):
            part[g][o // no, o % no] = mine_sums[o * cls_dev:(o + 1) * cls_dev, :]
        for k in range(1, ni):
            a_copy(g, k).start()

    chunk_sums(0)

    @pl.loop(1, no)
    def _(k):
        z_copy(k).wait()

    for k in range(1, ni):
        f_copy(k).start()

    for g in range(1, CHUNKS):
        chunk_sums(g)

    for r in range(RADII):
        padded[r * ODD:r * ODD + ANGLES, :] = flat_t[r * ANGLES:(r + 1) * ANGLES, :]
    for t in range(ANGLES):
        low = padded[pl.ds(t, RADII, stride=ODD), :].astype(jnp.bfloat16)
        for shift in range(2):
            for at in (t + shift + EXT, t + shift + EXT - ANGLES):
                if 0 <= at < ANGLES + EXT:
                    ptx[at * RADII:(at + 1) * RADII, shift * rows:(shift + 1) * rows] = low

    def second(g):
        for k in range(1, ni):
            a_copy(g, k).wait()
        acc = part[g][inner]
        for k in range(1, ni):
            acc = acc + gota[g][k]
        sums[g][...] = acc

        @pl.loop(1, no)
        def _(k):
            b_copy(g, k).start()

    second(0)

    for k in range(1, ni):
        i_copy(k).wait()
        f_copy(k).wait()

    for k in range(ni * no):
        for c in range(cls_dev):
            block = wire[k // no, k % no, c * WIRE:(c + 1) * WIRE, :].astype(jnp.float32)
            at = (k * cls_dev + c) * (WIRE + 1)
            wide[at:at + WIRE, :] = block
    for i in range(TILES):
        tile = wide[pl.ds(i, cls_count, stride=WIRE + 1), :].astype(jnp.bfloat16)
        for s1 in range(TURNS):
            at = (i - 3 * s1) % TILES
            rbig[s1 * cls_count:(s1 + 1) * cls_count, at * LANES:(at + 1) * LANES] = tile

    tops, mass = [], []
    for q in range(STEP // 2):
        at = (EXT - 2 * q) * RADII
        score = jnp.dot(rbig[...], ptx[at:at + FLAT, :], preferred_element_type=jnp.float32) * SCALE
        top = jnp.max(score, axis=0, keepdims=True)
        total = jnp.sum(jnp.exp(score - top), axis=0, keepdims=True)
        for h in range(2):
            tops.append(top[:, h * rows:(h + 1) * rows])
            mass.append(total[:, h * rows:(h + 1) * rows])
        if q + 1 < CHUNKS:
            second(q + 1)
    top = functools.reduce(jnp.maximum, tops)
    total = functools.reduce(jnp.add, [m * jnp.exp(t - top) for t, m in zip(tops, mass)])
    stat[0] = jnp.concatenate([top, total, jnp.zeros((6, rows), jnp.float32)], axis=0)
    stat_copy = core_copy(stat, 1)
    stat_copy.start()

    for g in range(CHUNKS):
        @pl.loop(1, no)
        def _(k):
            b_copy(g, k).wait()

        acc = sums[g][outer]
        for k in range(1, no):
            acc = acc + gotb[g][k]
        out_ref[:, g * CHUNK:(g + 1) * CHUNK] = acc[:, :CHUNK]
        if g == 0:
            out_ref[:, FLAT:FLAT + LANES] = acc[:, CHUNK:]

    stat_copy.wait()
    top2, total2 = stat[1, 0:1, :], stat[1, 1:2, :]
    high = jnp.maximum(top, top2)
    out = high + jnp.log(total * jnp.exp(top - high) + total2 * jnp.exp(top2 - high))
    out = jnp.where(grp == 0, out, jnp.concatenate([out[:, half:], out[:, :half]], axis=1))
    out_ref[:, FLAT + LANES:] = jnp.broadcast_to(out, (cls_dev, rows))


def finish(sums_ref, logev_ref, avg_ref):
    avg_ref[...] = sums_ref[:, :FLAT] / sums_ref[:, FLAT:FLAT + 1]
    logev_ref[...] = sums_ref[0:1, FLAT + LANES:FLAT + LANES + logev_ref.shape[1]]


def local(particles, references, classes, angles, weights):
    rows = particles.shape[0]
    half = rows // 2
    cls_dev = references.shape[0]
    n = lax.axis_size("loop")
    ni = INNER
    no = n // ni
    cls_count = n * cls_dev
    vmem = pl.BlockSpec(memory_space=pltpu.VMEM)
    f32, bf16 = jnp.float32, jnp.bfloat16

    def chunk_bufs(*lead):
        return [pltpu.VMEM((*lead, cls_dev, chunk_lanes(g)), f32) for g in range(CHUNKS)]

    dma = pltpu.SemaphoreType.DMA
    out = pl.pallas_call(
        functools.partial(kernel, ni, no, cls_dev),
        out_shape=jax.ShapeDtypeStruct((cls_dev, FLAT + LANES + rows), f32),
        in_specs=[vmem] * 5,
        out_specs=vmem,
        scratch_shapes=[
            pltpu.VMEM((LANES, LANES), f32),
            pltpu.VMEM((LANES, LANES), f32),
            pltpu.VMEM((cls_count * (WIRE + 1), LANES), f32),
            pltpu.VMEM((ni, no, cls_dev * WIRE, LANES), bf16),
            pltpu.VMEM((TURNS * cls_count, FLAT), bf16),
            pltpu.VMEM((2, 8, rows), jnp.int32),
            pltpu.VMEM((2, 8, rows), f32),
            pltpu.VMEM((FLAT, rows), f32),
            pltpu.VMEM((RADII * ODD, rows), f32),
            pltpu.VMEM((FLAT, rows), f32),
            pltpu.VMEM(((ANGLES + EXT) * RADII, 2 * rows), bf16),
            *chunk_bufs(ni, no), *chunk_bufs(ni, no), *chunk_bufs(no), *chunk_bufs(no),
            dma((no,)), dma((no,)), dma((ni,)), dma((ni,)), dma((ni,)), dma((ni,)),
            dma((CHUNKS, ni)), dma((CHUNKS, ni)), dma((CHUNKS, no)), dma((CHUNKS, no)),
            dma((2,)), dma((2,)),
        ],
        compiler_params=pltpu.CompilerParams(
            collective_id=0, has_side_effects=True, vmem_limit_bytes=(16 + n // 2) * 1024 * 1024),
    )(particles, references, classes.reshape(1, half), angles.reshape(1, half), weights.reshape(1, half))
    logev, avg = pl.pallas_call(
        finish,
        out_shape=(
            jax.ShapeDtypeStruct((1, half), f32),
            jax.ShapeDtypeStruct((cls_dev, FLAT), f32),
        ),
        in_specs=[vmem],
        out_specs=(vmem, vmem),
    )(out)
    return logev.reshape(half), avg


def solution(mesh):
    return jax.shard_map(
        local,
        mesh=mesh,
        in_specs=(
            P("loop", None),
            P(("loop", "grp"), None),
            P(("loop", "grp")),
            P(("loop", "grp")),
            P(("loop", "grp")),
        ),
        out_specs=(P(("loop", "grp")), P(("loop", "grp"), None)),
        check_vma=False,
    )
```

```python
import functools
import math

import jax
import jax.numpy as jnp
from jax import lax
from jax.experimental import pallas as pl
from jax.experimental.pallas import tpu as pltpu
from jax.sharding import PartitionSpec as P

RADII = 48
ANGLES = 72
FLAT = RADII * ANGLES
LANES = 128
TILES = FLAT // LANES
WIRE = 32
STEP = 8
TURNS = ANGLES // STEP
ODD = ANGLES + 1
EXT = STEP - 2
CHUNKS = 3
CHUNK_R = RADII // CHUNKS
CHUNK = FLAT // CHUNKS
INNER = 4
SCALE = 2.0 / math.sqrt(FLAT)
MESH = pl.DeviceIdType.MESH


def chunk_lanes(g):
    return CHUNK + (LANES if g == 0 else 0)


def kernel(
    ni, no, cls_dev,
    x_hbm, ref_hbm, cls_hbm, ang_hbm, wgt_hbm,
    out_ref,
    x_ref, ref_ref, cls_ref, ang_ref, wgt_ref, x_sem, in_sem,
    square, turned, wide, wire, rbig, lab, stat, flat_t, padded, flat_a, ptx,
    part0, part1, part2, gota0, gota1, gota2, sum0, sum1, sum2, gotb0, gotb1, gotb2,
    z_send, z_recv, i_send, i_recv, f_send, f_recv, a_send, a_recv, b_send, b_recv, c_send, c_recv,
):
    part, gota = (part0, part1, part2), (gota0, gota1, gota2)
    sums, gotb = (sum0, sum1, sum2), (gotb0, gotb1, gotb2)
    me = lax.axis_index("loop")
    grp = lax.axis_index("grp")
    outer, inner = me // ni, lax.rem(me, ni)
    rows = x_ref.shape[0]
    half = rows // 2
    cls_count = ni * no * cls_dev

    def outer_peer(k):
        return {"loop": lax.rem(outer + k, no) * ni + inner}

    def inner_peer(k):
        return {"loop": outer * ni + lax.rem(inner + k, ni)}

    other = {"grp": 1 - grp}

    def remote(src, dst, send, recv, to):
        return pltpu.make_async_remote_copy(
            src_ref=src, dst_ref=dst, send_sem=send, recv_sem=recv, device_id=to, device_id_type=MESH)

    def z_copy(k):
        return remote(wire.at[0, 0], wire.at[0, k], z_send.at[k], z_recv.at[k], outer_peer(k))

    def i_copy(k):
        return remote(wire.at[0, 0], wire.at[k, 0], i_send.at[k], i_recv.at[k], inner_peer(k))

    def f_copy(k):
        return remote(wire.at[0, 1:], wire.at[k, 1:], f_send.at[k], f_recv.at[k], inner_peer(k))

    def a_copy(g, k):
        return remote(part[g].at[lax.rem(inner + k, ni)], gota[g].at[k],
                      a_send.at[g, k], a_recv.at[g, k], inner_peer(k))

    def b_copy(g, k):
        return remote(sums[g].at[lax.rem(outer + k, no)], gotb[g].at[k],
                      b_send.at[g, k], b_recv.at[g, k], outer_peer(k))

    def core_copy(buf, k):
        return remote(buf.at[0], buf.at[1], c_send.at[k], c_recv.at[k], other)

    barrier = pltpu.get_barrier_semaphore()

    @pl.loop(1, no)
    def _(k):
        pl.semaphore_signal(barrier, inc=1, device_id=outer_peer(k), device_id_type=MESH)

    for k in range(1, ni):
        pl.semaphore_signal(barrier, inc=1, device_id=inner_peer(k), device_id_type=MESH)
    pl.semaphore_signal(barrier, inc=1, device_id=other, device_id_type=MESH)

    small = [pltpu.make_async_copy(src, dst, in_sem.at[i]) for i, (src, dst) in enumerate((
        (ref_hbm, ref_ref), (cls_hbm, cls_ref), (ang_hbm, ang_ref), (wgt_hbm, wgt_ref)))]
    for copy in small:
        copy.start()
    big = []
    for g in range(CHUNKS):
        sl = slice(g * CHUNK, (g + 1) * CHUNK)
        big.append(pltpu.make_async_copy(x_hbm.at[:, sl], x_ref.at[:, sl], x_sem.at[g]))
        big[-1].start()

    small[0].wait()
    refs = ref_ref[...].astype(jnp.float32)
    square[...] = jnp.zeros((LANES, LANES), jnp.float32)
    wide[0:cls_dev * WIRE, :] = jnp.zeros((cls_dev * WIRE, LANES), jnp.float32)
    for c in range(cls_dev):
        for r in range(RADII):
            square[r:r + 1, 0:ANGLES] = refs[c:c + 1, r * ANGLES:(r + 1) * ANGLES]
        turned[...] = square[...].T
        line = jnp.concatenate(
            [turned[pl.ds(v, TURNS, stride=STEP), :][:, 0:RADII] for v in range(STEP)], axis=1)
        for w in range(3):
            wide[pl.ds(c * WIRE + w, TURNS, stride=3), :] = line[:, w * LANES:(w + 1) * LANES]
    wire[0, 0] = wide[0:cls_dev * WIRE, :].astype(jnp.bfloat16)

    for copy in small[1:]:
        copy.wait()
    lane = lax.broadcasted_iota(jnp.int32, (1, rows), 1)
    mine = (lane // half) == grp
    lab[0] = jnp.zeros((8, rows), jnp.int32)
    for i, src in enumerate((cls_ref, ang_ref, wgt_ref)):
        both = jnp.concatenate([src[...], src[...]], axis=1)
        lab[0, i:i + 1, :] = jnp.where(mine, both, 0)

    def transpose(g):
        big[g].wait()
        for i in range(g * (CHUNK // LANES), (g + 1) * (CHUNK // LANES)):
            tile = x_ref[:, i * LANES:(i + 1) * LANES].T
            flat_t[i * LANES:(i + 1) * LANES, :] = tile.astype(jnp.float32)

    transpose(0)
    pl.semaphore_wait(barrier, ni + no - 1)

    label_copy = core_copy(lab, 0)
    label_copy.start()

    @pl.loop(1, no)
    def _(k):
        z_copy(k).start()

    for k in range(1, ni):
        i_copy(k).start()

    transpose(1)
    transpose(2)

    label_copy.wait()
    labels = lab[0] + lab[1]
    classes, angles, weights = labels[0:1], labels[1:2], labels[2:3]
    bits = [jnp.broadcast_to(((angles >> b) & 1) == 1, (8, rows)) for b in range(7)]

    row = lax.broadcasted_iota(jnp.int32, (cls_count, rows), 0)
    owner = row // cls_dev
    named = (((owner % no) * ni + owner // no) * 2 + grp) * cls_dev + row % cls_dev
    pick = jnp.where(named == classes, weights, 0).astype(jnp.float32).astype(jnp.bfloat16)

    sub = lax.broadcasted_iota(jnp.int32, (8, rows), 0)

    def chunk_sums(g):
        for r in range(g * CHUNK_R, (g + 1) * CHUNK_R):
            base = r * ANGLES
            vals = [flat_t[base + STEP * u:base + STEP * (u + 1), :] for u in range(TURNS)]
            for b in range(4):
                vals = [jnp.where(bits[3 + b], vals[(u - (1 << b)) % TURNS], vals[u])
                        for u in range(TURNS)]
            for b in range(3):
                by = 1 << b
                moved = [pltpu.roll(v, by, 0) for v in vals]
                vals = [jnp.where(bits[b], jnp.where(sub < by, moved[(u - 1) % TURNS], moved[u]), vals[u])
                        for u in range(TURNS)]
            for u in range(TURNS):
                flat_a[base + STEP * u:base + STEP * (u + 1), :] = vals[u]
        aligned = flat_a[g * CHUNK:(g + 1) * CHUNK, :].astype(jnp.bfloat16)
        if g == 0:
            aligned = jnp.concatenate([aligned, jnp.ones((LANES, rows), jnp.bfloat16)], axis=0)
        mine_sums = lax.dot_general(pick, aligned, (((1,), (1,)), ((), ())),
                                    preferred_element_type=jnp.float32)
        for o in range(ni * no):
            part[g][o // no, o % no] = mine_sums[o * cls_dev:(o + 1) * cls_dev, :]
        for k in range(1, ni):
            a_copy(g, k).start()

    chunk_sums(0)

    @pl.loop(1, no)
    def _(k):
        z_copy(k).wait()

    for k in range(1, ni):
        f_copy(k).start()

    for g in range(1, CHUNKS):
        chunk_sums(g)

    for r in range(RADII):
        padded[r * ODD:r * ODD + ANGLES, :] = flat_t[r * ANGLES:(r + 1) * ANGLES, :]
    for t in range(ANGLES):
        low = padded[pl.ds(t, RADII, stride=ODD), :].astype(jnp.bfloat16)
        for shift in range(2):
            for at in (t + shift + EXT, t + shift + EXT - ANGLES):
                if 0 <= at < ANGLES + EXT:
                    ptx[at * RADII:(at + 1) * RADII, shift * rows:(shift + 1) * rows] = low

    def second(g):
        for k in range(1, ni):
            a_copy(g, k).wait()
        acc = part[g][inner]
        for k in range(1, ni):
            acc = acc + gota[g][k]
        sums[g][...] = acc

        @pl.loop(1, no)
        def _(k):
            b_copy(g, k).start()

    second(0)

    for k in range(1, ni):
        i_copy(k).wait()
        f_copy(k).wait()

    for k in range(ni * no):
        for c in range(cls_dev):
            block = wire[k // no, k % no, c * WIRE:(c + 1) * WIRE, :].astype(jnp.float32)
            at = (k * cls_dev + c) * (WIRE + 1)
            wide[at:at + WIRE, :] = block
    for i in range(TILES):
        tile = wide[pl.ds(i, cls_count, stride=WIRE + 1), :].astype(jnp.bfloat16)
        for s1 in range(TURNS):
            at = (i - 3 * s1) % TILES
            rbig[s1 * cls_count:(s1 + 1) * cls_count, at * LANES:(at + 1) * LANES] = tile

    tops, mass = [], []
    for q in range(STEP // 2):
        at = (EXT - 2 * q) * RADII
        score = jnp.dot(rbig[...], ptx[at:at + FLAT, :], preferred_element_type=jnp.float32) * SCALE
        top = jnp.max(score, axis=0, keepdims=True)
        total = jnp.sum(jnp.exp(score - top), axis=0, keepdims=True)
        for h in range(2):
            tops.append(top[:, h * rows:(h + 1) * rows])
            mass.append(total[:, h * rows:(h + 1) * rows])
        if q + 1 < CHUNKS:
            second(q + 1)
    top = functools.reduce(jnp.maximum, tops)
    total = functools.reduce(jnp.add, [m * jnp.exp(t - top) for t, m in zip(tops, mass)])
    stat[0] = jnp.concatenate([top, total, jnp.zeros((6, rows), jnp.float32)], axis=0)
    stat_copy = core_copy(stat, 1)
    stat_copy.start()

    for g in range(CHUNKS):
        @pl.loop(1, no)
        def _(k):
            b_copy(g, k).wait()

        acc = sums[g][outer]
        for k in range(1, no):
            acc = acc + gotb[g][k]
        out_ref[:, g * CHUNK:(g + 1) * CHUNK] = acc[:, :CHUNK]
        if g == 0:
            out_ref[:, FLAT:FLAT + LANES] = acc[:, CHUNK:]

    stat_copy.wait()
    top2, total2 = stat[1, 0:1, :], stat[1, 1:2, :]
    high = jnp.maximum(top, top2)
    out = high + jnp.log(total * jnp.exp(top - high) + total2 * jnp.exp(top2 - high))
    out = jnp.where(grp == 0, out, jnp.concatenate([out[:, half:], out[:, :half]], axis=1))
    out_ref[:, FLAT + LANES:] = jnp.broadcast_to(out, (cls_dev, rows))


def finish(sums_ref, logev_ref, avg_ref):
    avg_ref[...] = sums_ref[:, :FLAT] / sums_ref[:, FLAT:FLAT + 1]
    logev_ref[...] = sums_ref[0:1, FLAT + LANES:FLAT + LANES + logev_ref.shape[1]]


def local(particles, references, classes, angles, weights):
    rows = particles.shape[0]
    half = rows // 2
    cls_dev = references.shape[0]
    n = lax.axis_size("loop")
    ni = INNER
    no = n // ni
    cls_count = n * cls_dev
    vmem = pl.BlockSpec(memory_space=pltpu.VMEM)
    f32, bf16 = jnp.float32, jnp.bfloat16

    def chunk_bufs(*lead):
        return [pltpu.VMEM((*lead, cls_dev, chunk_lanes(g)), f32) for g in range(CHUNKS)]

    dma = pltpu.SemaphoreType.DMA
    out = pl.pallas_call(
        functools.partial(kernel, ni, no, cls_dev),
        out_shape=jax.ShapeDtypeStruct((cls_dev, FLAT + LANES + rows), f32),
        in_specs=[pl.BlockSpec(memory_space=pltpu.HBM)] * 5,
        out_specs=vmem,
        scratch_shapes=[
            pltpu.VMEM((rows, FLAT), bf16),
            pltpu.VMEM((cls_dev, FLAT), bf16),
            pltpu.VMEM((1, half), jnp.int32),
            pltpu.VMEM((1, half), jnp.int32),
            pltpu.VMEM((1, half), jnp.int32),
            dma((CHUNKS,)),
            dma((4,)),
            pltpu.VMEM((LANES, LANES), f32),
            pltpu.VMEM((LANES, LANES), f32),
            pltpu.VMEM((cls_count * (WIRE + 1), LANES), f32),
            pltpu.VMEM((ni, no, cls_dev * WIRE, LANES), bf16),
            pltpu.VMEM((TURNS * cls_count, FLAT), bf16),
            pltpu.VMEM((2, 8, rows), jnp.int32),
            pltpu.VMEM((2, 8, rows), f32),
            pltpu.VMEM((FLAT, rows), f32),
            pltpu.VMEM((RADII * ODD, rows), f32),
            pltpu.VMEM((FLAT, rows), f32),
            pltpu.VMEM(((ANGLES + EXT) * RADII, 2 * rows), bf16),
            *chunk_bufs(ni, no), *chunk_bufs(ni, no), *chunk_bufs(no), *chunk_bufs(no),
            dma((no,)), dma((no,)), dma((ni,)), dma((ni,)), dma((ni,)), dma((ni,)),
            dma((CHUNKS, ni)), dma((CHUNKS, ni)), dma((CHUNKS, no)), dma((CHUNKS, no)),
            dma((2,)), dma((2,)),
        ],
        compiler_params=pltpu.CompilerParams(
            collective_id=0, has_side_effects=True, vmem_limit_bytes=56 * 1024 * 1024),
    )(particles, references, classes.reshape(1, half), angles.reshape(1, half), weights.reshape(1, half))
    logev, avg = pl.pallas_call(
        finish,
        out_shape=(
            jax.ShapeDtypeStruct((1, half), f32),
            jax.ShapeDtypeStruct((cls_dev, FLAT), f32),
        ),
        in_specs=[vmem],
        out_specs=(vmem, vmem),
        compiler_params=pltpu.CompilerParams(vmem_limit_bytes=2 * 1024 * 1024),
    )(out)
    return logev.reshape(half), avg


def solution(mesh):
    return jax.shard_map(
        local,
        mesh=mesh,
        in_specs=(
            P("loop", None),
            P(("loop", "grp"), None),
            P(("loop", "grp")),
            P(("loop", "grp")),
            P(("loop", "grp")),
        ),
        out_specs=(P(("loop", "grp")), P(("loop", "grp"), None)),
        check_vma=False,
    )
```

```python
import functools
import math

import jax
import jax.numpy as jnp
from jax import lax
from jax.experimental import pallas as pl
from jax.experimental.pallas import tpu as pltpu
from jax.sharding import PartitionSpec as P

RADII = 48
ANGLES = 72
FLAT = RADII * ANGLES
LANES = 128
TILES = FLAT // LANES
WIRE = 32
STEP = 8
TURNS = ANGLES // STEP
ODD = ANGLES + 1
EXT = STEP - 2
CHUNKS = 3
CHUNK_R = RADII // CHUNKS
CHUNK = FLAT // CHUNKS
INNER = 4
SCALE = 2.0 / math.sqrt(FLAT)
MESH = pl.DeviceIdType.MESH


def chunk_lanes(g):
    return CHUNK + (LANES if g == 0 else 0)


def kernel(
    ni, no, cls_dev,
    x_hbm, ref_hbm, cls_hbm, ang_hbm, wgt_hbm,
    out_ref,
    x_ref, ref_ref, cls_ref, ang_ref, wgt_ref, x_sem, in_sem,
    square, turned, wide, wire, rbig, lab, stat, flat_t, padded, flat_a, ptx,
    part0, part1, part2, gota0, gota1, gota2, sum0, sum1, sum2, gotb0, gotb1, gotb2,
    z_send, z_recv, i_send, i_recv, f_send, f_recv, a_send, a_recv, b_send, b_recv, c_send, c_recv,
):
    part, gota = (part0, part1, part2), (gota0, gota1, gota2)
    sums, gotb = (sum0, sum1, sum2), (gotb0, gotb1, gotb2)
    me = lax.axis_index("loop")
    grp = lax.axis_index("grp")
    outer, inner = me // ni, lax.rem(me, ni)
    rows = x_ref.shape[0]
    half = rows // 2
    cls_count = ni * no * cls_dev

    def outer_peer(k):
        return {"loop": lax.rem(outer + k, no) * ni + inner}

    def inner_peer(k):
        return {"loop": outer * ni + lax.rem(inner + k, ni)}

    other = {"grp": 1 - grp}

    def remote(src, dst, send, recv, to):
        return pltpu.make_async_remote_copy(
            src_ref=src, dst_ref=dst, send_sem=send, recv_sem=recv, device_id=to, device_id_type=MESH)

    def z_copy(k):
        return remote(wire.at[0, 0], wire.at[0, k], z_send.at[k], z_recv.at[k], outer_peer(k))

    def i_copy(k):
        return remote(wire.at[0, 0], wire.at[k, 0], i_send.at[k], i_recv.at[k], inner_peer(k))

    def f_copy(k):
        return remote(wire.at[0, 1:], wire.at[k, 1:], f_send.at[k], f_recv.at[k], inner_peer(k))

    def a_copy(g, k):
        return remote(part[g].at[lax.rem(inner + k, ni)], gota[g].at[k],
                      a_send.at[g, k], a_recv.at[g, k], inner_peer(k))

    def b_copy(g, k):
        return remote(sums[g].at[lax.rem(outer + k, no)], gotb[g].at[k],
                      b_send.at[g, k], b_recv.at[g, k], outer_peer(k))

    def core_copy(buf, k):
        return remote(buf.at[0], buf.at[1], c_send.at[k], c_recv.at[k], other)

    barrier = pltpu.get_barrier_semaphore()

    for k in range(1, no):
        pl.semaphore_signal(barrier, inc=1, device_id=outer_peer(k), device_id_type=MESH)

    for k in range(1, ni):
        pl.semaphore_signal(barrier, inc=1, device_id=inner_peer(k), device_id_type=MESH)
    pl.semaphore_signal(barrier, inc=1, device_id=other, device_id_type=MESH)

    small = [pltpu.make_async_copy(src, dst, in_sem.at[i]) for i, (src, dst) in enumerate((
        (ref_hbm, ref_ref), (cls_hbm, cls_ref), (ang_hbm, ang_ref), (wgt_hbm, wgt_ref)))]
    for copy in small:
        copy.start()
    big = []
    for g in range(CHUNKS):
        sl = slice(g * CHUNK, (g + 1) * CHUNK)
        big.append(pltpu.make_async_copy(x_hbm.at[:, sl], x_ref.at[:, sl], x_sem.at[g]))
        big[-1].start()

    small[0].wait()
    refs = ref_ref[...].astype(jnp.float32)
    square[...] = jnp.zeros((LANES, LANES), jnp.float32)
    wide[0:cls_dev * WIRE, :] = jnp.zeros((cls_dev * WIRE, LANES), jnp.float32)
    for c in range(cls_dev):
        for r in range(RADII):
            square[r:r + 1, 0:ANGLES] = refs[c:c + 1, r * ANGLES:(r + 1) * ANGLES]
        turned[...] = square[...].T
        line = jnp.concatenate(
            [turned[pl.ds(v, TURNS, stride=STEP), :][:, 0:RADII] for v in range(STEP)], axis=1)
        for w in range(3):
            wide[pl.ds(c * WIRE + w, TURNS, stride=3), :] = line[:, w * LANES:(w + 1) * LANES]
    wire[0, 0] = wide[0:cls_dev * WIRE, :].astype(jnp.bfloat16)

    for copy in small[1:]:
        copy.wait()
    lane = lax.broadcasted_iota(jnp.int32, (1, rows), 1)
    mine = (lane // half) == grp
    lab[0] = jnp.zeros((8, rows), jnp.int32)
    for i, src in enumerate((cls_ref, ang_ref, wgt_ref)):
        both = jnp.concatenate([src[...], src[...]], axis=1)
        lab[0, i:i + 1, :] = jnp.where(mine, both, 0)

    def transpose(g):
        big[g].wait()
        for i in range(g * (CHUNK // LANES), (g + 1) * (CHUNK // LANES)):
            tile = x_ref[:, i * LANES:(i + 1) * LANES].T
            flat_t[i * LANES:(i + 1) * LANES, :] = tile.astype(jnp.float32)

    transpose(0)
    pl.semaphore_wait(barrier, ni + no - 1)

    label_copy = core_copy(lab, 0)
    label_copy.start()

    for k in range(1, no):
        z_copy(k).start()

    for k in range(1, ni):
        i_copy(k).start()

    transpose(1)
    transpose(2)

    label_copy.wait()
    labels = lab[0] + lab[1]
    classes, angles, weights = labels[0:1], labels[1:2], labels[2:3]
    bits = [jnp.broadcast_to(((angles >> b) & 1) == 1, (8, rows)) for b in range(7)]

    row = lax.broadcasted_iota(jnp.int32, (cls_count, rows), 0)
    owner = row // cls_dev
    named = (((owner % no) * ni + owner // no) * 2 + grp) * cls_dev + row % cls_dev
    pick = jnp.where(named == classes, weights, 0).astype(jnp.float32).astype(jnp.bfloat16)

    sub = lax.broadcasted_iota(jnp.int32, (8, rows), 0)

    def chunk_sums(g):
        for r in range(g * CHUNK_R, (g + 1) * CHUNK_R):
            base = r * ANGLES
            vals = [flat_t[base + STEP * u:base + STEP * (u + 1), :] for u in range(TURNS)]
            for b in range(4):
                vals = [jnp.where(bits[3 + b], vals[(u - (1 << b)) % TURNS], vals[u])
                        for u in range(TURNS)]
            for b in range(3):
                by = 1 << b
                moved = [pltpu.roll(v, by, 0) for v in vals]
                vals = [jnp.where(bits[b], jnp.where(sub < by, moved[(u - 1) % TURNS], moved[u]), vals[u])
                        for u in range(TURNS)]
            for u in range(TURNS):
                flat_a[base + STEP * u:base + STEP * (u + 1), :] = vals[u]
        aligned = flat_a[g * CHUNK:(g + 1) * CHUNK, :].astype(jnp.bfloat16)
        if g == 0:
            aligned = jnp.concatenate([aligned, jnp.ones((LANES, rows), jnp.bfloat16)], axis=0)
        mine_sums = lax.dot_general(pick, aligned, (((1,), (1,)), ((), ())),
                                    preferred_element_type=jnp.float32)
        per = no * cls_dev
        for i in range(ni):
            part[g][i] = mine_sums[i * per:(i + 1) * per, :]
        for k in range(1, ni):
            a_copy(g, k).start()

    chunk_sums(0)

    for k in range(1, no):
        z_copy(k).wait()

    for k in range(1, ni):
        f_copy(k).start()

    for g in range(1, CHUNKS):
        chunk_sums(g)

    for r in range(RADII):
        padded[r * ODD:r * ODD + ANGLES, :] = flat_t[r * ANGLES:(r + 1) * ANGLES, :]
    for t in range(ANGLES):
        low = padded[pl.ds(t, RADII, stride=ODD), :].astype(jnp.bfloat16)
        for shift in range(2):
            for at in (t + shift + EXT, t + shift + EXT - ANGLES):
                if 0 <= at < ANGLES + EXT:
                    ptx[at * RADII:(at + 1) * RADII, shift * rows:(shift + 1) * rows] = low

    def second(g):
        for k in range(1, ni):
            a_copy(g, k).wait()
        acc = part[g][inner]
        for k in range(1, ni):
            acc = acc + gota[g][k]
        for z in range(no):
            sums[g][z] = acc[z * cls_dev:(z + 1) * cls_dev, :]
        for k in range(1, no):
            b_copy(g, k).start()

    second(0)

    for k in range(1, ni):
        i_copy(k).wait()
        f_copy(k).wait()

    for k in range(ni * no):
        for c in range(cls_dev):
            block = wire[k // no, k % no, c * WIRE:(c + 1) * WIRE, :].astype(jnp.float32)
            at = (k * cls_dev + c) * (WIRE + 1)
            wide[at:at + WIRE, :] = block
    for i in range(TILES):
        tile = wide[pl.ds(i, cls_count, stride=WIRE + 1), :].astype(jnp.bfloat16)
        for s1 in range(TURNS):
            at = (i - 3 * s1) % TILES
            rbig[s1 * cls_count:(s1 + 1) * cls_count, at * LANES:(at + 1) * LANES] = tile

    tops, mass = [], []
    for q in range(STEP // 2):
        at = (EXT - 2 * q) * RADII
        score = jnp.dot(rbig[...], ptx[at:at + FLAT, :], preferred_element_type=jnp.float32) * SCALE
        top = jnp.max(score, axis=0, keepdims=True)
        total = jnp.sum(jnp.exp(score - top), axis=0, keepdims=True)
        for h in range(2):
            tops.append(top[:, h * rows:(h + 1) * rows])
            mass.append(total[:, h * rows:(h + 1) * rows])
        if q == 1:
            for g in range(1, CHUNKS):
                second(g)
    top = functools.reduce(jnp.maximum, tops)
    total = functools.reduce(jnp.add, [m * jnp.exp(t - top) for t, m in zip(tops, mass)])
    stat[0] = jnp.concatenate([top, total, jnp.zeros((6, rows), jnp.float32)], axis=0)
    stat_copy = core_copy(stat, 1)
    stat_copy.start()

    for g in range(CHUNKS):
        for k in range(1, no):
            b_copy(g, k).wait()

        acc = sums[g][outer]
        for k in range(1, no):
            acc = acc + gotb[g][k]
        out_ref[:, g * CHUNK:(g + 1) * CHUNK] = acc[:, :CHUNK]
        if g == 0:
            out_ref[:, FLAT:FLAT + LANES] = acc[:, CHUNK:]

    stat_copy.wait()
    top2, total2 = stat[1, 0:1, :], stat[1, 1:2, :]
    high = jnp.maximum(top, top2)
    out = high + jnp.log(total * jnp.exp(top - high) + total2 * jnp.exp(top2 - high))
    out = jnp.where(grp == 0, out, jnp.concatenate([out[:, half:], out[:, :half]], axis=1))
    out_ref[:, FLAT + LANES:] = jnp.broadcast_to(out, (cls_dev, rows))


def finish(sums_ref, logev_ref, avg_ref):
    avg_ref[...] = sums_ref[:, :FLAT] / sums_ref[:, FLAT:FLAT + 1]
    logev_ref[...] = sums_ref[0:1, FLAT + LANES:FLAT + LANES + logev_ref.shape[1]]


def local(particles, references, classes, angles, weights):
    rows = particles.shape[0]
    half = rows // 2
    cls_dev = references.shape[0]
    n = lax.axis_size("loop")
    ni = INNER
    no = n // ni
    cls_count = n * cls_dev
    vmem = pl.BlockSpec(memory_space=pltpu.VMEM)
    f32, bf16 = jnp.float32, jnp.bfloat16

    def chunk_bufs(*lead):
        return [pltpu.VMEM((*lead, chunk_lanes(g)), f32) for g in range(CHUNKS)]

    dma = pltpu.SemaphoreType.DMA
    out = pl.pallas_call(
        functools.partial(kernel, ni, no, cls_dev),
        out_shape=pltpu.VMEM((cls_dev, FLAT + LANES + rows), f32),
        in_specs=[pl.BlockSpec(memory_space=pltpu.HBM)] * 5,
        out_specs=vmem,
        scratch_shapes=[
            pltpu.VMEM((rows, FLAT), bf16),
            pltpu.VMEM((cls_dev, FLAT), bf16),
            pltpu.VMEM((1, half), jnp.int32),
            pltpu.VMEM((1, half), jnp.int32),
            pltpu.VMEM((1, half), jnp.int32),
            dma((CHUNKS,)),
            dma((4,)),
            pltpu.VMEM((LANES, LANES), f32),
            pltpu.VMEM((LANES, LANES), f32),
            pltpu.VMEM((cls_count * (WIRE + 1), LANES), f32),
            pltpu.VMEM((ni, no, cls_dev * WIRE, LANES), bf16),
            pltpu.VMEM((TURNS * cls_count, FLAT), bf16),
            pltpu.VMEM((2, 8, rows), jnp.int32),
            pltpu.VMEM((2, 8, rows), f32),
            pltpu.VMEM((FLAT, rows), f32),
            pltpu.VMEM((RADII * ODD, rows), f32),
            pltpu.VMEM((FLAT, rows), f32),
            pltpu.VMEM(((ANGLES + EXT) * RADII, 2 * rows), bf16),
            *chunk_bufs(ni, no * cls_dev), *chunk_bufs(ni, no * cls_dev),
            *chunk_bufs(no, cls_dev), *chunk_bufs(no, cls_dev),
            dma((no,)), dma((no,)), dma((ni,)), dma((ni,)), dma((ni,)), dma((ni,)),
            dma((CHUNKS, ni)), dma((CHUNKS, ni)), dma((CHUNKS, no)), dma((CHUNKS, no)),
            dma((2,)), dma((2,)),
        ],
        compiler_params=pltpu.CompilerParams(
            collective_id=0, has_side_effects=True, vmem_limit_bytes=56 * 1024 * 1024),
    )(particles, references, classes.reshape(1, half), angles.reshape(1, half), weights.reshape(1, half))
    logev, avg = pl.pallas_call(
        finish,
        out_shape=(
            jax.ShapeDtypeStruct((1, half), f32),
            jax.ShapeDtypeStruct((cls_dev, FLAT), f32),
        ),
        in_specs=[vmem],
        out_specs=(vmem, vmem),
        compiler_params=pltpu.CompilerParams(vmem_limit_bytes=2 * 1024 * 1024),
    )(out)
    return logev.reshape(half), avg


def solution(mesh):
    return jax.shard_map(
        local,
        mesh=mesh,
        in_specs=(
            P("loop", None),
            P(("loop", "grp"), None),
            P(("loop", "grp")),
            P(("loop", "grp")),
            P(("loop", "grp")),
        ),
        out_specs=(P(("loop", "grp")), P(("loop", "grp"), None)),
        check_vma=False,
    )
```

```python
import functools
import math

import jax
import jax.numpy as jnp
from jax import lax
from jax.experimental import pallas as pl
from jax.experimental.pallas import tpu as pltpu
from jax.sharding import PartitionSpec as P

RADII = 48
ANGLES = 72
FLAT = RADII * ANGLES
LANES = 128
TILES = FLAT // LANES
WIRE = 32
STEP = 8
TURNS = ANGLES // STEP
ODD = ANGLES + 1
EXT = STEP - 2
CORES = 2
FETCHES = 3
FETCH = FLAT // FETCHES
CORE_R = RADII // CORES
CORE_FLAT = CORE_R * ANGLES
CHUNKS = ((0, 16), (16, 8))
ONES = LANES // 2
CORE_LANES = CORE_FLAT + ONES
INNER = 4
SCALE = 2.0 / math.sqrt(FLAT)
MESH = pl.DeviceIdType.MESH


def chunk_lanes(g):
    return CHUNKS[g][1] * ANGLES + (ONES if g + 1 == len(CHUNKS) else 0)


def kernel(
    ni, no, cls_dev,
    x_hbm, ref_hbm, cls_hbm, ang_hbm, wgt_hbm,
    out_ref,
    x_ref, ref_ref, cls_ref, ang_ref, wgt_ref, x_sem, in_sem,
    square, turned, wide, wire, rbig, lab, stat, flat_t, padded, flat_a, ptx,
    part0, part1, gota0, gota1, sum0, sum1, gotb0, gotb1, keep, swap,
    z_send, z_recv, i_send, i_recv, f_send, f_recv, a_send, a_recv, b_send, b_recv, c_send, c_recv,
):
    part, gota, sums, gotb = (part0, part1), (gota0, gota1), (sum0, sum1), (gotb0, gotb1)
    me = lax.axis_index("loop")
    grp = lax.axis_index("grp")
    outer, inner = me // ni, lax.rem(me, ni)
    rows = x_ref.shape[0]
    half = rows // 2
    cls_count = ni * no * cls_dev

    def outer_peer(k):
        return {"loop": lax.rem(outer + k, no) * ni + inner}

    def inner_peer(k):
        return {"loop": outer * ni + lax.rem(inner + k, ni)}

    other = {"grp": 1 - grp}

    def remote(src, dst, send, recv, to):
        return pltpu.make_async_remote_copy(
            src_ref=src, dst_ref=dst, send_sem=send, recv_sem=recv, device_id=to, device_id_type=MESH)

    def z_copy(k):
        return remote(wire.at[0, 0], wire.at[0, k], z_send.at[k], z_recv.at[k], outer_peer(k))

    def i_copy(k):
        return remote(wire.at[0, 0], wire.at[k, 0], i_send.at[k], i_recv.at[k], inner_peer(k))

    def f_copy(k):
        return remote(wire.at[0, 1:], wire.at[k, 1:], f_send.at[k], f_recv.at[k], inner_peer(k))

    def a_copy(g, k):
        return remote(part[g].at[lax.rem(inner + k, ni)], gota[g].at[k],
                      a_send.at[g, k], a_recv.at[g, k], inner_peer(k))

    def b_copy(g, k):
        return remote(sums[g].at[lax.rem(outer + k, no)], gotb[g].at[k],
                      b_send.at[g, k], b_recv.at[g, k], outer_peer(k))

    def core_copy(buf, k):
        return remote(buf.at[0], buf.at[1], c_send.at[k], c_recv.at[k], other)

    barrier = pltpu.get_barrier_semaphore()

    for k in range(1, no):
        pl.semaphore_signal(barrier, inc=1, device_id=outer_peer(k), device_id_type=MESH)

    for k in range(1, ni):
        pl.semaphore_signal(barrier, inc=1, device_id=inner_peer(k), device_id_type=MESH)
    pl.semaphore_signal(barrier, inc=1, device_id=other, device_id_type=MESH)

    small = [pltpu.make_async_copy(src, dst, in_sem.at[i]) for i, (src, dst) in enumerate((
        (ref_hbm, ref_ref), (cls_hbm, cls_ref), (ang_hbm, ang_ref), (wgt_hbm, wgt_ref)))]
    for copy in small:
        copy.start()
    big = []
    for g in range(FETCHES):
        sl = slice(g * FETCH, (g + 1) * FETCH)
        big.append(pltpu.make_async_copy(x_hbm.at[:, sl], x_ref.at[:, sl], x_sem.at[g]))
        big[-1].start()

    small[0].wait()
    refs = ref_ref[...].astype(jnp.float32)
    square[...] = jnp.zeros((LANES, LANES), jnp.float32)
    wide[0:cls_dev * WIRE, :] = jnp.zeros((cls_dev * WIRE, LANES), jnp.float32)
    for c in range(cls_dev):
        for r in range(RADII):
            square[r:r + 1, 0:ANGLES] = refs[c:c + 1, r * ANGLES:(r + 1) * ANGLES]
        turned[...] = square[...].T
        line = jnp.concatenate(
            [turned[pl.ds(v, TURNS, stride=STEP), :][:, 0:RADII] for v in range(STEP)], axis=1)
        for w in range(3):
            wide[pl.ds(c * WIRE + w, TURNS, stride=3), :] = line[:, w * LANES:(w + 1) * LANES]
    wire[0, 0] = wide[0:cls_dev * WIRE, :].astype(jnp.bfloat16)

    for copy in small[1:]:
        copy.wait()
    lane = lax.broadcasted_iota(jnp.int32, (1, rows), 1)
    mine = (lane // half) == grp
    lab[0] = jnp.zeros((8, rows), jnp.int32)
    for i, src in enumerate((cls_ref, ang_ref, wgt_ref)):
        both = jnp.concatenate([src[...], src[...]], axis=1)
        lab[0, i:i + 1, :] = jnp.where(mine, both, 0)

    def transpose(g):
        big[g].wait()
        for i in range(g * (FETCH // LANES), (g + 1) * (FETCH // LANES)):
            tile = x_ref[:, i * LANES:(i + 1) * LANES].T
            flat_t[i * LANES:(i + 1) * LANES, :] = tile.astype(jnp.float32)

    pl.semaphore_wait(barrier, ni + no - 1)

    label_copy = core_copy(lab, 0)
    label_copy.start()

    for k in range(1, no):
        z_copy(k).start()

    for k in range(1, ni):
        i_copy(k).start()

    for g in range(FETCHES):
        transpose(g)

    label_copy.wait()
    labels = lab[0] + lab[1]
    classes, angles, weights = labels[0:1], labels[1:2], labels[2:3]
    bits = [jnp.broadcast_to(((angles >> b) & 1) == 1, (8, rows)) for b in range(7)]

    own_cls = CORES * cls_dev
    per = no * own_cls
    row = lax.broadcasted_iota(jnp.int32, (ni * per, rows), 0)
    owner = row // own_cls
    named = ((owner % no) * ni + owner // no) * own_cls + row % own_cls
    pick = jnp.where(named == classes, weights, 0).astype(jnp.float32).astype(jnp.bfloat16)
    sub = lax.broadcasted_iota(jnp.int32, (8, rows), 0)

    def chunk_sums(g):
        first, count = CHUNKS[g]
        for r in range(first, first + count):
            base = r * ANGLES
            vals = [flat_t[pl.ds(pl.multiple_of(grp * CORE_FLAT + base + STEP * u, STEP), STEP), :]
                    for u in range(TURNS)]
            for b in range(4):
                vals = [jnp.where(bits[3 + b], vals[(u - (1 << b)) % TURNS], vals[u])
                        for u in range(TURNS)]
            for b in range(3):
                by = 1 << b
                moved = [pltpu.roll(v, by, 0) for v in vals]
                vals = [jnp.where(bits[b], jnp.where(sub < by, moved[(u - 1) % TURNS], moved[u]), vals[u])
                        for u in range(TURNS)]
            for u in range(TURNS):
                flat_a[base + STEP * u:base + STEP * (u + 1), :] = vals[u]
        aligned = flat_a[first * ANGLES:(first + count) * ANGLES, :].astype(jnp.bfloat16)
        if g + 1 == len(CHUNKS):
            aligned = jnp.concatenate([aligned, jnp.ones((ONES, rows), jnp.bfloat16)], axis=0)
        mine_sums = lax.dot_general(pick, aligned, (((1,), (1,)), ((), ())),
                                    preferred_element_type=jnp.float32)
        for i in range(ni):
            part[g][i] = mine_sums[i * per:(i + 1) * per, :]
        for k in range(1, ni):
            a_copy(g, k).start()

    chunk_sums(0)

    for k in range(1, no):
        z_copy(k).wait()

    for k in range(1, ni):
        f_copy(k).start()

    for g in range(1, len(CHUNKS)):
        chunk_sums(g)

    for r in range(RADII):
        padded[r * ODD:r * ODD + ANGLES, :] = flat_t[r * ANGLES:(r + 1) * ANGLES, :]
    for t in range(ANGLES):
        low = padded[pl.ds(t, RADII, stride=ODD), :].astype(jnp.bfloat16)
        for shift in range(2):
            for at in (t + shift + EXT, t + shift + EXT - ANGLES):
                if 0 <= at < ANGLES + EXT:
                    ptx[at * RADII:(at + 1) * RADII, shift * rows:(shift + 1) * rows] = low

    def second(g):
        for k in range(1, ni):
            a_copy(g, k).wait()
        acc = part[g][inner]
        for k in range(1, ni):
            acc = acc + gota[g][k]
        for z in range(no):
            sums[g][z] = acc[z * own_cls:(z + 1) * own_cls, :]
        for k in range(1, no):
            b_copy(g, k).start()

    second(0)

    for k in range(1, ni):
        i_copy(k).wait()
        f_copy(k).wait()

    for k in range(ni * no):
        for c in range(cls_dev):
            block = wire[k // no, k % no, c * WIRE:(c + 1) * WIRE, :].astype(jnp.float32)
            at = (k * cls_dev + c) * (WIRE + 1)
            wide[at:at + WIRE, :] = block
    for i in range(TILES):
        tile = wide[pl.ds(i, cls_count, stride=WIRE + 1), :].astype(jnp.bfloat16)
        for s1 in range(TURNS):
            at = (i - 3 * s1) % TILES
            rbig[s1 * cls_count:(s1 + 1) * cls_count, at * LANES:(at + 1) * LANES] = tile

    tops, mass = [], []
    for q in range(STEP // 2):
        at = (EXT - 2 * q) * RADII
        score = jnp.dot(rbig[...], ptx[at:at + FLAT, :], preferred_element_type=jnp.float32) * SCALE
        top = jnp.max(score, axis=0, keepdims=True)
        total = jnp.sum(jnp.exp(score - top), axis=0, keepdims=True)
        for h in range(2):
            tops.append(top[:, h * rows:(h + 1) * rows])
            mass.append(total[:, h * rows:(h + 1) * rows])
        if q == 1:
            for g in range(1, len(CHUNKS)):
                second(g)
    top = functools.reduce(jnp.maximum, tops)
    total = functools.reduce(jnp.add, [m * jnp.exp(t - top) for t, m in zip(tops, mass)])
    stat[0] = jnp.concatenate([top, total, jnp.zeros((6, rows), jnp.float32)], axis=0)
    stat_copy = core_copy(stat, 1)
    stat_copy.start()

    for g in range(len(CHUNKS)):
        for k in range(1, no):
            b_copy(g, k).wait()
        acc = sums[g][outer]
        for k in range(1, no):
            acc = acc + gotb[g][k]
        low, high = acc[:cls_dev], acc[cls_dev:]
        at = CHUNKS[g][0] * ANGLES
        keep[:, at:at + chunk_lanes(g)] = jnp.where(grp == 0, low, high)
        swap[0, :, at:at + chunk_lanes(g)] = jnp.where(grp == 0, high, low)
    swap_copy = core_copy(swap, 2)
    swap_copy.start()

    stat_copy.wait()
    top2, total2 = stat[1, 0:1, :], stat[1, 1:2, :]
    high = jnp.maximum(top, top2)
    out = high + jnp.log(total * jnp.exp(top - high) + total2 * jnp.exp(top2 - high))
    out = jnp.where(grp == 0, out, jnp.concatenate([out[:, half:], out[:, :half]], axis=1))
    out_ref[:, FLAT + LANES:] = jnp.broadcast_to(out, (cls_dev, rows))

    swap_copy.wait()
    own, theirs = keep[...], swap[1]
    out_ref[:, :CORE_FLAT] = jnp.where(grp == 0, own, theirs)[:, :CORE_FLAT]
    out_ref[:, CORE_FLAT:FLAT] = jnp.where(grp == 0, theirs, own)[:, :CORE_FLAT]
    out_ref[:, FLAT:FLAT + LANES] = own[:, CORE_LANES - LANES:]


def finish(sums_ref, logev_ref, avg_ref):
    avg_ref[...] = sums_ref[:, :FLAT] / sums_ref[:, FLAT + ONES:FLAT + ONES + 1]
    logev_ref[...] = sums_ref[0:1, FLAT + LANES:FLAT + LANES + logev_ref.shape[1]]


def local(particles, references, classes, angles, weights):
    rows = particles.shape[0]
    half = rows // 2
    cls_dev = references.shape[0]
    n = lax.axis_size("loop")
    ni = INNER
    no = n // ni
    cls_count = n * cls_dev
    own_cls = CORES * cls_dev
    vmem = pl.BlockSpec(memory_space=pltpu.VMEM)
    f32, bf16 = jnp.float32, jnp.bfloat16

    def chunk_bufs(*lead):
        return [pltpu.VMEM((*lead, chunk_lanes(g)), f32) for g in range(len(CHUNKS))]

    dma = pltpu.SemaphoreType.DMA
    out = pl.pallas_call(
        functools.partial(kernel, ni, no, cls_dev),
        out_shape=pltpu.VMEM((cls_dev, FLAT + LANES + rows), f32),
        in_specs=[pl.BlockSpec(memory_space=pltpu.HBM)] * 5,
        out_specs=vmem,
        scratch_shapes=[
            pltpu.VMEM((rows, FLAT), bf16),
            pltpu.VMEM((cls_dev, FLAT), bf16),
            pltpu.VMEM((1, half), jnp.int32),
            pltpu.VMEM((1, half), jnp.int32),
            pltpu.VMEM((1, half), jnp.int32),
            dma((FETCHES,)),
            dma((4,)),
            pltpu.VMEM((LANES, LANES), f32),
            pltpu.VMEM((LANES, LANES), f32),
            pltpu.VMEM((cls_count * (WIRE + 1), LANES), f32),
            pltpu.VMEM((ni, no, cls_dev * WIRE, LANES), bf16),
            pltpu.VMEM((TURNS * cls_count, FLAT), bf16),
            pltpu.VMEM((2, 8, rows), jnp.int32),
            pltpu.VMEM((2, 8, rows), f32),
            pltpu.VMEM((FLAT, rows), f32),
            pltpu.VMEM((RADII * ODD, rows), f32),
            pltpu.VMEM((CORE_FLAT, rows), f32),
            pltpu.VMEM(((ANGLES + EXT) * RADII, 2 * rows), bf16),
            *chunk_bufs(ni, no * own_cls), *chunk_bufs(ni, no * own_cls),
            *chunk_bufs(no, own_cls), *chunk_bufs(no, own_cls),
            pltpu.VMEM((cls_dev, CORE_LANES), f32), pltpu.VMEM((2, cls_dev, CORE_LANES), f32),
            dma((no,)), dma((no,)), dma((ni,)), dma((ni,)), dma((ni,)), dma((ni,)),
            dma((len(CHUNKS), ni)), dma((len(CHUNKS), ni)), dma((len(CHUNKS), no)), dma((len(CHUNKS), no)),
            dma((3,)), dma((3,)),
        ],
        compiler_params=pltpu.CompilerParams(
            collective_id=0, has_side_effects=True, vmem_limit_bytes=56 * 1024 * 1024),
    )(particles, references, classes.reshape(1, half), angles.reshape(1, half), weights.reshape(1, half))
    logev, avg = pl.pallas_call(
        finish,
        out_shape=(
            jax.ShapeDtypeStruct((1, half), f32),
            jax.ShapeDtypeStruct((cls_dev, FLAT), f32),
        ),
        in_specs=[vmem],
        out_specs=(vmem, vmem),
        compiler_params=pltpu.CompilerParams(vmem_limit_bytes=2 * 1024 * 1024),
    )(out)
    return logev.reshape(half), avg


def solution(mesh):
    return jax.shard_map(
        local,
        mesh=mesh,
        in_specs=(
            P("loop", None),
            P(("loop", "grp"), None),
            P(("loop", "grp")),
            P(("loop", "grp")),
            P(("loop", "grp")),
        ),
        out_specs=(P(("loop", "grp")), P(("loop", "grp"), None)),
        check_vma=False,
    )
```

```python
import functools
import math

import jax
import jax.numpy as jnp
from jax import lax
from jax.experimental import pallas as pl
from jax.experimental.pallas import tpu as pltpu
from jax.sharding import PartitionSpec as P

RADII = 48
ANGLES = 72
FLAT = RADII * ANGLES
LANES = 128
TILES = FLAT // LANES
WIRE = 32
STEP = 8
TURNS = ANGLES // STEP
ODD = ANGLES + 1
EXT = STEP - 2
CHUNKS = 3
CHUNK_R = RADII // CHUNKS
CHUNK = FLAT // CHUNKS
INNER = 4
SCALE = 2.0 / math.sqrt(FLAT)
MESH = pl.DeviceIdType.MESH


def chunk_lanes(g):
    return CHUNK + (LANES if g == 0 else 0)


def kernel(
    ni, no, cls_dev,
    x_hbm, ref_hbm, cls_hbm, ang_hbm, wgt_hbm,
    out_ref,
    x_ref, ref_ref, cls_ref, ang_ref, wgt_ref, x_sem, in_sem,
    square, turned, wide, wire, rbig, lab, stat, flat_t, padded, flat_a, ptx,
    part0, part1, part2, gota0, gota1, gota2, sum0, sum1, sum2, gotb0, gotb1, gotb2,
    z_send, z_recv, i_send, i_recv, f_send, f_recv, a_send, a_recv, b_send, b_recv, c_send, c_recv,
):
    part, gota = (part0, part1, part2), (gota0, gota1, gota2)
    sums, gotb = (sum0, sum1, sum2), (gotb0, gotb1, gotb2)
    me = lax.axis_index("loop")
    grp = lax.axis_index("grp")
    outer, inner = me // ni, lax.rem(me, ni)
    rows = x_ref.shape[0]
    half = rows // 2
    cls_count = ni * no * cls_dev

    def outer_peer(k):
        return {"loop": lax.rem(outer + k, no) * ni + inner}

    def inner_peer(k):
        return {"loop": outer * ni + lax.rem(inner + k, ni)}

    other = {"grp": 1 - grp}

    def remote(src, dst, send, recv, to):
        return pltpu.make_async_remote_copy(
            src_ref=src, dst_ref=dst, send_sem=send, recv_sem=recv, device_id=to, device_id_type=MESH)

    def z_copy(k):
        return remote(wire.at[0, 0], wire.at[0, k], z_send.at[k], z_recv.at[k], outer_peer(k))

    def i_copy(k):
        return remote(wire.at[0, 0], wire.at[k, 0], i_send.at[k], i_recv.at[k], inner_peer(k))

    def f_copy(k):
        return remote(wire.at[0, 1:], wire.at[k, 1:], f_send.at[k], f_recv.at[k], inner_peer(k))

    def a_copy(g, k):
        return remote(part[g].at[lax.rem(inner + k, ni)], gota[g].at[k],
                      a_send.at[g, k], a_recv.at[g, k], inner_peer(k))

    def b_copy(g, k):
        return remote(sums[g].at[lax.rem(outer + k, no)], gotb[g].at[k],
                      b_send.at[g, k], b_recv.at[g, k], outer_peer(k))

    def core_copy(buf, k):
        return remote(buf.at[0], buf.at[1], c_send.at[k], c_recv.at[k], other)

    barrier = pltpu.get_barrier_semaphore()

    for k in range(1, no):
        pl.semaphore_signal(barrier, inc=1, device_id=outer_peer(k), device_id_type=MESH)

    for k in range(1, ni):
        pl.semaphore_signal(barrier, inc=1, device_id=inner_peer(k), device_id_type=MESH)
    pl.semaphore_signal(barrier, inc=1, device_id=other, device_id_type=MESH)

    small = [pltpu.make_async_copy(src, dst, in_sem.at[i]) for i, (src, dst) in enumerate((
        (ref_hbm, ref_ref), (cls_hbm, cls_ref), (ang_hbm, ang_ref), (wgt_hbm, wgt_ref)))]
    for copy in small:
        copy.start()
    big = []
    for g in range(CHUNKS):
        sl = slice(g * CHUNK, (g + 1) * CHUNK)
        big.append(pltpu.make_async_copy(x_hbm.at[:, sl], x_ref.at[:, sl], x_sem.at[g]))
        big[-1].start()

    for copy in small[1:]:
        copy.wait()
    lane = lax.broadcasted_iota(jnp.int32, (1, rows), 1)
    mine = (lane // half) == grp
    lab[0] = jnp.zeros((8, rows), jnp.int32)
    for i, src in enumerate((cls_ref, ang_ref, wgt_ref)):
        both = jnp.concatenate([src[...], src[...]], axis=1)
        lab[0, i:i + 1, :] = jnp.where(mine, both, 0)

    pl.semaphore_wait(barrier, ni + no - 1)

    label_copy = core_copy(lab, 0)
    label_copy.start()

    small[0].wait()
    refs = ref_ref[...].astype(jnp.float32)
    square[...] = jnp.zeros((LANES, LANES), jnp.float32)
    wide[0:cls_dev * WIRE, :] = jnp.zeros((cls_dev * WIRE, LANES), jnp.float32)
    for c in range(cls_dev):
        for r in range(RADII):
            square[r:r + 1, 0:ANGLES] = refs[c:c + 1, r * ANGLES:(r + 1) * ANGLES]
        turned[...] = square[...].T
        line = jnp.concatenate(
            [turned[pl.ds(v, TURNS, stride=STEP), :][:, 0:RADII] for v in range(STEP)], axis=1)
        for w in range(3):
            wide[pl.ds(c * WIRE + w, TURNS, stride=3), :] = line[:, w * LANES:(w + 1) * LANES]
    wire[0, 0] = wide[0:cls_dev * WIRE, :].astype(jnp.bfloat16)

    def transpose(g):
        big[g].wait()
        for i in range(g * (CHUNK // LANES), (g + 1) * (CHUNK // LANES)):
            tile = x_ref[:, i * LANES:(i + 1) * LANES].T
            flat_t[i * LANES:(i + 1) * LANES, :] = tile.astype(jnp.float32)

    for k in range(1, no):
        z_copy(k).start()

    for k in range(1, ni):
        i_copy(k).start()

    transpose(0)

    label_copy.wait()
    labels = lab[0] + lab[1]
    classes, angles, weights = labels[0:1], labels[1:2], labels[2:3]
    bits = [jnp.broadcast_to(((angles >> b) & 1) == 1, (8, rows)) for b in range(7)]

    row = lax.broadcasted_iota(jnp.int32, (cls_count, rows), 0)
    owner = row // cls_dev
    named = (((owner % no) * ni + owner // no) * 2 + grp) * cls_dev + row % cls_dev
    pick = jnp.where(named == classes, weights, 0).astype(jnp.float32).astype(jnp.bfloat16)

    sub = lax.broadcasted_iota(jnp.int32, (8, rows), 0)

    def chunk_sums(g):
        for r in range(g * CHUNK_R, (g + 1) * CHUNK_R):
            base = r * ANGLES
            vals = [flat_t[base + STEP * u:base + STEP * (u + 1), :] for u in range(TURNS)]
            for b in range(4):
                vals = [jnp.where(bits[3 + b], vals[(u - (1 << b)) % TURNS], vals[u])
                        for u in range(TURNS)]
            for b in range(3):
                by = 1 << b
                moved = [pltpu.roll(v, by, 0) for v in vals]
                vals = [jnp.where(bits[b], jnp.where(sub < by, moved[(u - 1) % TURNS], moved[u]), vals[u])
                        for u in range(TURNS)]
            for u in range(TURNS):
                flat_a[base + STEP * u:base + STEP * (u + 1), :] = vals[u]
        aligned = flat_a[g * CHUNK:(g + 1) * CHUNK, :].astype(jnp.bfloat16)
        if g == 0:
            aligned = jnp.concatenate([aligned, jnp.ones((LANES, rows), jnp.bfloat16)], axis=0)
        mine_sums = lax.dot_general(pick, aligned, (((1,), (1,)), ((), ())),
                                    preferred_element_type=jnp.float32)
        per = no * cls_dev
        for i in range(ni):
            part[g][i] = mine_sums[i * per:(i + 1) * per, :]
        for k in range(1, ni):
            a_copy(g, k).start()

    chunk_sums(0)

    for k in range(1, no):
        z_copy(k).wait()

    for k in range(1, ni):
        f_copy(k).start()

    for g in range(1, CHUNKS):
        transpose(g)
        chunk_sums(g)

    for r in range(RADII):
        padded[r * ODD:r * ODD + ANGLES, :] = flat_t[r * ANGLES:(r + 1) * ANGLES, :]
    for t in range(ANGLES):
        low = padded[pl.ds(t, RADII, stride=ODD), :].astype(jnp.bfloat16)
        for shift in range(2):
            for at in (t + shift + EXT, t + shift + EXT - ANGLES):
                if 0 <= at < ANGLES + EXT:
                    ptx[at * RADII:(at + 1) * RADII, shift * rows:(shift + 1) * rows] = low

    def second(g):
        for k in range(1, ni):
            a_copy(g, k).wait()
        acc = part[g][inner]
        for k in range(1, ni):
            acc = acc + gota[g][k]
        for z in range(no):
            sums[g][z] = acc[z * cls_dev:(z + 1) * cls_dev, :]
        for k in range(1, no):
            b_copy(g, k).start()

    second(0)

    for k in range(1, ni):
        i_copy(k).wait()
        f_copy(k).wait()

    for k in range(ni * no):
        for c in range(cls_dev):
            block = wire[k // no, k % no, c * WIRE:(c + 1) * WIRE, :].astype(jnp.float32)
            at = (k * cls_dev + c) * (WIRE + 1)
            wide[at:at + WIRE, :] = block
    for i in range(TILES):
        tile = wide[pl.ds(i, cls_count, stride=WIRE + 1), :].astype(jnp.bfloat16)
        for s1 in range(TURNS):
            at = (i - 3 * s1) % TILES
            rbig[s1 * cls_count:(s1 + 1) * cls_count, at * LANES:(at + 1) * LANES] = tile

    tops, mass = [], []
    for q in range(STEP // 2):
        at = (EXT - 2 * q) * RADII
        score = jnp.dot(rbig[...], ptx[at:at + FLAT, :], preferred_element_type=jnp.float32) * SCALE
        top = jnp.max(score, axis=0, keepdims=True)
        total = jnp.sum(jnp.exp(score - top), axis=0, keepdims=True)
        for h in range(2):
            tops.append(top[:, h * rows:(h + 1) * rows])
            mass.append(total[:, h * rows:(h + 1) * rows])
        if 1 <= q < CHUNKS:
            second(q)
    top = functools.reduce(jnp.maximum, tops)
    total = functools.reduce(jnp.add, [m * jnp.exp(t - top) for t, m in zip(tops, mass)])
    stat[0] = jnp.concatenate([top, total, jnp.zeros((6, rows), jnp.float32)], axis=0)
    stat_copy = core_copy(stat, 1)
    stat_copy.start()

    for g in range(CHUNKS):
        for k in range(1, no):
            b_copy(g, k).wait()

        acc = sums[g][outer]
        for k in range(1, no):
            acc = acc + gotb[g][k]
        out_ref[:, g * CHUNK:(g + 1) * CHUNK] = acc[:, :CHUNK]
        if g == 0:
            out_ref[:, FLAT:FLAT + LANES] = acc[:, CHUNK:]

    stat_copy.wait()
    top2, total2 = stat[1, 0:1, :], stat[1, 1:2, :]
    high = jnp.maximum(top, top2)
    out = high + jnp.log(total * jnp.exp(top - high) + total2 * jnp.exp(top2 - high))
    out = jnp.where(grp == 0, out, jnp.concatenate([out[:, half:], out[:, :half]], axis=1))
    out_ref[:, FLAT + LANES:] = jnp.broadcast_to(out, (cls_dev, rows))


def finish(sums_ref, logev_ref, avg_ref):
    avg_ref[...] = sums_ref[:, :FLAT] / sums_ref[:, FLAT:FLAT + 1]
    logev_ref[...] = sums_ref[0:1, FLAT + LANES:FLAT + LANES + logev_ref.shape[1]]


def local(particles, references, classes, angles, weights):
    rows = particles.shape[0]
    half = rows // 2
    cls_dev = references.shape[0]
    n = lax.axis_size("loop")
    ni = INNER
    no = n // ni
    cls_count = n * cls_dev
    vmem = pl.BlockSpec(memory_space=pltpu.VMEM)
    f32, bf16 = jnp.float32, jnp.bfloat16

    def chunk_bufs(*lead):
        return [pltpu.VMEM((*lead, chunk_lanes(g)), f32) for g in range(CHUNKS)]

    dma = pltpu.SemaphoreType.DMA
    out = pl.pallas_call(
        functools.partial(kernel, ni, no, cls_dev),
        out_shape=pltpu.VMEM((cls_dev, FLAT + LANES + rows), f32),
        in_specs=[pl.BlockSpec(memory_space=pltpu.HBM)] * 5,
        out_specs=vmem,
        scratch_shapes=[
            pltpu.VMEM((rows, FLAT), bf16),
            pltpu.VMEM((cls_dev, FLAT), bf16),
            pltpu.VMEM((1, half), jnp.int32),
            pltpu.VMEM((1, half), jnp.int32),
            pltpu.VMEM((1, half), jnp.int32),
            dma((CHUNKS,)),
            dma((4,)),
            pltpu.VMEM((LANES, LANES), f32),
            pltpu.VMEM((LANES, LANES), f32),
            pltpu.VMEM((cls_count * (WIRE + 1), LANES), f32),
            pltpu.VMEM((ni, no, cls_dev * WIRE, LANES), bf16),
            pltpu.VMEM((TURNS * cls_count, FLAT), bf16),
            pltpu.VMEM((2, 8, rows), jnp.int32),
            pltpu.VMEM((2, 8, rows), f32),
            pltpu.VMEM((FLAT, rows), f32),
            pltpu.VMEM((RADII * ODD, rows), f32),
            pltpu.VMEM((FLAT, rows), f32),
            pltpu.VMEM(((ANGLES + EXT) * RADII, 2 * rows), bf16),
            *chunk_bufs(ni, no * cls_dev), *chunk_bufs(ni, no * cls_dev),
            *chunk_bufs(no, cls_dev), *chunk_bufs(no, cls_dev),
            dma((no,)), dma((no,)), dma((ni,)), dma((ni,)), dma((ni,)), dma((ni,)),
            dma((CHUNKS, ni)), dma((CHUNKS, ni)), dma((CHUNKS, no)), dma((CHUNKS, no)),
            dma((2,)), dma((2,)),
        ],
        compiler_params=pltpu.CompilerParams(
            collective_id=0, has_side_effects=True, vmem_limit_bytes=56 * 1024 * 1024),
    )(particles, references, classes.reshape(1, half), angles.reshape(1, half), weights.reshape(1, half))
    logev, avg = pl.pallas_call(
        finish,
        out_shape=(
            jax.ShapeDtypeStruct((1, half), f32),
            jax.ShapeDtypeStruct((cls_dev, FLAT), f32),
        ),
        in_specs=[vmem],
        out_specs=(vmem, vmem),
        compiler_params=pltpu.CompilerParams(vmem_limit_bytes=2 * 1024 * 1024),
    )(out)
    return logev.reshape(half), avg


def solution(mesh):
    return jax.shard_map(
        local,
        mesh=mesh,
        in_specs=(
            P("loop", None),
            P(("loop", "grp"), None),
            P(("loop", "grp")),
            P(("loop", "grp")),
            P(("loop", "grp")),
        ),
        out_specs=(P(("loop", "grp")), P(("loop", "grp"), None)),
        check_vma=False,
    )
```

```python
import functools
import math

import jax
import jax.numpy as jnp
from jax import lax
from jax.experimental import pallas as pl
from jax.experimental.pallas import tpu as pltpu
from jax.sharding import PartitionSpec as P

RADII = 48
ANGLES = 72
FLAT = RADII * ANGLES
LANES = 128
TILES = FLAT // LANES
WIRE = 32
STEP = 8
TURNS = ANGLES // STEP
ODD = ANGLES + 1
EXT = STEP - 2
CHUNKS = 3
CHUNK_R = RADII // CHUNKS
CHUNK = FLAT // CHUNKS
INNER = 4
SCALE = 2.0 / math.sqrt(FLAT)
MESH = pl.DeviceIdType.MESH


def chunk_lanes(g):
    return CHUNK + (LANES if g == 0 else 0)


def kernel(
    ni, no, cls_dev,
    x_hbm, ref_hbm, cls_hbm, ang_hbm, wgt_hbm,
    out_ref,
    x_ref, ref_ref, cls_ref, ang_ref, wgt_ref, x_sem, in_sem,
    square, turned, wide, wire, rbig, lab, stat, flat_t, padded, flat_a, ptx,
    part0, part1, part2, gota0, gota1, gota2, sum0, sum1, sum2, gotb0, gotb1, gotb2,
    z_send, z_recv, i_send, i_recv, f_send, f_recv, a_send, a_recv, b_send, b_recv, c_send, c_recv,
):
    part, gota = (part0, part1, part2), (gota0, gota1, gota2)
    sums, gotb = (sum0, sum1, sum2), (gotb0, gotb1, gotb2)
    me = lax.axis_index("loop")
    grp = lax.axis_index("grp")
    outer, inner = me // ni, lax.rem(me, ni)
    rows = x_ref.shape[0]
    half = rows // 2
    cls_count = ni * no * cls_dev

    def outer_peer(k):
        return {"loop": lax.rem(outer + k, no) * ni + inner}

    def inner_peer(k):
        return {"loop": outer * ni + lax.rem(inner + k, ni)}

    other = {"grp": 1 - grp}

    def remote(src, dst, send, recv, to):
        return pltpu.make_async_remote_copy(
            src_ref=src, dst_ref=dst, send_sem=send, recv_sem=recv, device_id=to, device_id_type=MESH)

    def z_copy(k):
        return remote(wire.at[0, 0], wire.at[0, k], z_send.at[k], z_recv.at[k], outer_peer(k))

    def i_copy(k):
        return remote(wire.at[0, 0], wire.at[k, 0], i_send.at[k], i_recv.at[k], inner_peer(k))

    def f_copy(k):
        return remote(wire.at[0, 1:], wire.at[k, 1:], f_send.at[k], f_recv.at[k], inner_peer(k))

    def a_copy(g, k):
        return remote(part[g].at[lax.rem(inner + k, ni)], gota[g].at[k],
                      a_send.at[g, k], a_recv.at[g, k], inner_peer(k))

    def b_copy(g, k):
        return remote(sums[g].at[lax.rem(outer + k, no)], gotb[g].at[k],
                      b_send.at[g, k], b_recv.at[g, k], outer_peer(k))

    def core_copy(buf, k):
        return remote(buf.at[0], buf.at[1], c_send.at[k], c_recv.at[k], other)

    barrier = pltpu.get_barrier_semaphore()

    for k in range(1, no):
        pl.semaphore_signal(barrier, inc=1, device_id=outer_peer(k), device_id_type=MESH)

    for k in range(1, ni):
        pl.semaphore_signal(barrier, inc=1, device_id=inner_peer(k), device_id_type=MESH)
    pl.semaphore_signal(barrier, inc=1, device_id=other, device_id_type=MESH)

    small = [pltpu.make_async_copy(src, dst, in_sem.at[i]) for i, (src, dst) in enumerate((
        (ref_hbm, ref_ref), (cls_hbm, cls_ref), (ang_hbm, ang_ref), (wgt_hbm, wgt_ref)))]
    for copy in small:
        copy.start()
    big = []
    for g in range(CHUNKS):
        sl = slice(g * CHUNK, (g + 1) * CHUNK)
        big.append(pltpu.make_async_copy(x_hbm.at[:, sl], x_ref.at[:, sl], x_sem.at[g]))
        big[-1].start()

    small[0].wait()
    refs = ref_ref[...].astype(jnp.float32)
    square[...] = jnp.zeros((LANES, LANES), jnp.float32)
    wide[0:cls_dev * WIRE, :] = jnp.zeros((cls_dev * WIRE, LANES), jnp.float32)
    for c in range(cls_dev):
        for r in range(RADII):
            square[r:r + 1, 0:ANGLES] = refs[c:c + 1, r * ANGLES:(r + 1) * ANGLES]
        turned[...] = square[...].T
        line = jnp.concatenate(
            [turned[pl.ds(v, TURNS, stride=STEP), :][:, 0:RADII] for v in range(STEP)], axis=1)
        for w in range(3):
            wide[pl.ds(c * WIRE + w, TURNS, stride=3), :] = line[:, w * LANES:(w + 1) * LANES]
    wire[0, 0] = wide[0:cls_dev * WIRE, :].astype(jnp.bfloat16)

    for copy in small[1:]:
        copy.wait()
    lane = lax.broadcasted_iota(jnp.int32, (1, rows), 1)
    mine = (lane // half) == grp
    lab[0] = jnp.zeros((8, rows), jnp.int32)
    for i, src in enumerate((cls_ref, ang_ref, wgt_ref)):
        both = jnp.concatenate([src[...], src[...]], axis=1)
        lab[0, i:i + 1, :] = jnp.where(mine, both, 0)

    def transpose(g):
        big[g].wait()
        for i in range(g * (CHUNK // LANES), (g + 1) * (CHUNK // LANES)):
            tile = x_ref[:, i * LANES:(i + 1) * LANES].T
            flat_t[i * LANES:(i + 1) * LANES, :] = tile.astype(jnp.float32)

    transpose(0)
    pl.semaphore_wait(barrier, ni + no - 1)

    label_copy = core_copy(lab, 0)
    label_copy.start()

    for k in range(1, no):
        z_copy(k).start()

    for k in range(1, ni):
        i_copy(k).start()

    transpose(1)
    transpose(2)

    label_copy.wait()
    for k in range(1, no):
        z_copy(k).wait()

    for k in range(1, ni):
        f_copy(k).start()

    labels = lab[0] + lab[1]
    classes, angles, weights = labels[0:1], labels[1:2], labels[2:3]
    bits = [jnp.broadcast_to(((angles >> b) & 1) == 1, (8, rows)) for b in range(7)]

    row = lax.broadcasted_iota(jnp.int32, (cls_count, rows), 0)
    owner = row // cls_dev
    named = (((owner % no) * ni + owner // no) * 2 + grp) * cls_dev + row % cls_dev
    pick = jnp.where(named == classes, weights, 0).astype(jnp.float32).astype(jnp.bfloat16)

    sub = lax.broadcasted_iota(jnp.int32, (8, rows), 0)

    def chunk_sums(g):
        for r in range(g * CHUNK_R, (g + 1) * CHUNK_R):
            base = r * ANGLES
            vals = [flat_t[base + STEP * u:base + STEP * (u + 1), :] for u in range(TURNS)]
            for b in range(4):
                vals = [jnp.where(bits[3 + b], vals[(u - (1 << b)) % TURNS], vals[u])
                        for u in range(TURNS)]
            for b in range(3):
                by = 1 << b
                moved = [pltpu.roll(v, by, 0) for v in vals]
                vals = [jnp.where(bits[b], jnp.where(sub < by, moved[(u - 1) % TURNS], moved[u]), vals[u])
                        for u in range(TURNS)]
            for u in range(TURNS):
                flat_a[base + STEP * u:base + STEP * (u + 1), :] = vals[u]
        aligned = flat_a[g * CHUNK:(g + 1) * CHUNK, :].astype(jnp.bfloat16)
        if g == 0:
            aligned = jnp.concatenate([aligned, jnp.ones((LANES, rows), jnp.bfloat16)], axis=0)
        mine_sums = lax.dot_general(pick, aligned, (((1,), (1,)), ((), ())),
                                    preferred_element_type=jnp.float32)
        per = no * cls_dev
        for i in range(ni):
            part[g][i] = mine_sums[i * per:(i + 1) * per, :]
        for k in range(1, ni):
            a_copy(g, k).start()

    chunk_sums(0)

    for g in range(1, CHUNKS):
        chunk_sums(g)

    for r in range(RADII):
        padded[r * ODD:r * ODD + ANGLES, :] = flat_t[r * ANGLES:(r + 1) * ANGLES, :]
    for t in range(ANGLES):
        low = padded[pl.ds(t, RADII, stride=ODD), :].astype(jnp.bfloat16)
        for shift in range(2):
            for at in (t + shift + EXT, t + shift + EXT - ANGLES):
                if 0 <= at < ANGLES + EXT:
                    ptx[at * RADII:(at + 1) * RADII, shift * rows:(shift + 1) * rows] = low

    def second(g):
        for k in range(1, ni):
            a_copy(g, k).wait()
        acc = part[g][inner]
        for k in range(1, ni):
            acc = acc + gota[g][k]
        for z in range(no):
            sums[g][z] = acc[z * cls_dev:(z + 1) * cls_dev, :]
        for k in range(1, no):
            b_copy(g, k).start()

    second(0)

    for k in range(1, ni):
        i_copy(k).wait()
        f_copy(k).wait()

    for k in range(ni * no):
        for c in range(cls_dev):
            block = wire[k // no, k % no, c * WIRE:(c + 1) * WIRE, :].astype(jnp.float32)
            at = (k * cls_dev + c) * (WIRE + 1)
            wide[at:at + WIRE, :] = block
    for i in range(TILES):
        tile = wide[pl.ds(i, cls_count, stride=WIRE + 1), :].astype(jnp.bfloat16)
        for s1 in range(TURNS):
            at = (i - 3 * s1) % TILES
            rbig[s1 * cls_count:(s1 + 1) * cls_count, at * LANES:(at + 1) * LANES] = tile

    tops, mass = [], []
    for q in range(STEP // 2):
        at = (EXT - 2 * q) * RADII
        score = jnp.dot(rbig[...], ptx[at:at + FLAT, :], preferred_element_type=jnp.float32) * SCALE
        top = jnp.max(score, axis=0, keepdims=True)
        total = jnp.sum(jnp.exp(score - top), axis=0, keepdims=True)
        for h in range(2):
            tops.append(top[:, h * rows:(h + 1) * rows])
            mass.append(total[:, h * rows:(h + 1) * rows])
        if q == 1:
            for g in range(1, CHUNKS):
                second(g)
    top = functools.reduce(jnp.maximum, tops)
    total = functools.reduce(jnp.add, [m * jnp.exp(t - top) for t, m in zip(tops, mass)])
    stat[0] = jnp.concatenate([top, total, jnp.zeros((6, rows), jnp.float32)], axis=0)
    stat_copy = core_copy(stat, 1)
    stat_copy.start()

    for g in range(CHUNKS):
        for k in range(1, no):
            b_copy(g, k).wait()

        acc = sums[g][outer]
        for k in range(1, no):
            acc = acc + gotb[g][k]
        out_ref[:, g * CHUNK:(g + 1) * CHUNK] = acc[:, :CHUNK]
        if g == 0:
            out_ref[:, FLAT:FLAT + LANES] = acc[:, CHUNK:]

    stat_copy.wait()
    top2, total2 = stat[1, 0:1, :], stat[1, 1:2, :]
    high = jnp.maximum(top, top2)
    out = high + jnp.log(total * jnp.exp(top - high) + total2 * jnp.exp(top2 - high))
    out = jnp.where(grp == 0, out, jnp.concatenate([out[:, half:], out[:, :half]], axis=1))
    out_ref[:, FLAT + LANES:] = jnp.broadcast_to(out, (cls_dev, rows))


def finish(sums_ref, logev_ref, avg_ref):
    avg_ref[...] = sums_ref[:, :FLAT] / sums_ref[:, FLAT:FLAT + 1]
    logev_ref[...] = sums_ref[0:1, FLAT + LANES:FLAT + LANES + logev_ref.shape[1]]


def local(particles, references, classes, angles, weights):
    rows = particles.shape[0]
    half = rows // 2
    cls_dev = references.shape[0]
    n = lax.axis_size("loop")
    ni = INNER
    no = n // ni
    cls_count = n * cls_dev
    vmem = pl.BlockSpec(memory_space=pltpu.VMEM)
    f32, bf16 = jnp.float32, jnp.bfloat16

    def chunk_bufs(*lead):
        return [pltpu.VMEM((*lead, chunk_lanes(g)), f32) for g in range(CHUNKS)]

    dma = pltpu.SemaphoreType.DMA
    out = pl.pallas_call(
        functools.partial(kernel, ni, no, cls_dev),
        out_shape=pltpu.VMEM((cls_dev, FLAT + LANES + rows), f32),
        in_specs=[pl.BlockSpec(memory_space=pltpu.HBM)] * 5,
        out_specs=vmem,
        scratch_shapes=[
            pltpu.VMEM((rows, FLAT), bf16),
            pltpu.VMEM((cls_dev, FLAT), bf16),
            pltpu.VMEM((1, half), jnp.int32),
            pltpu.VMEM((1, half), jnp.int32),
            pltpu.VMEM((1, half), jnp.int32),
            dma((CHUNKS,)),
            dma((4,)),
            pltpu.VMEM((LANES, LANES), f32),
            pltpu.VMEM((LANES, LANES), f32),
            pltpu.VMEM((cls_count * (WIRE + 1), LANES), f32),
            pltpu.VMEM((ni, no, cls_dev * WIRE, LANES), bf16),
            pltpu.VMEM((TURNS * cls_count, FLAT), bf16),
            pltpu.VMEM((2, 8, rows), jnp.int32),
            pltpu.VMEM((2, 8, rows), f32),
            pltpu.VMEM((FLAT, rows), f32),
            pltpu.VMEM((RADII * ODD, rows), f32),
            pltpu.VMEM((FLAT, rows), f32),
            pltpu.VMEM(((ANGLES + EXT) * RADII, 2 * rows), bf16),
            *chunk_bufs(ni, no * cls_dev), *chunk_bufs(ni, no * cls_dev),
            *chunk_bufs(no, cls_dev), *chunk_bufs(no, cls_dev),
            dma((no,)), dma((no,)), dma((ni,)), dma((ni,)), dma((ni,)), dma((ni,)),
            dma((CHUNKS, ni)), dma((CHUNKS, ni)), dma((CHUNKS, no)), dma((CHUNKS, no)),
            dma((2,)), dma((2,)),
        ],
        compiler_params=pltpu.CompilerParams(
            collective_id=0, has_side_effects=True, vmem_limit_bytes=56 * 1024 * 1024),
    )(particles, references, classes.reshape(1, half), angles.reshape(1, half), weights.reshape(1, half))
    logev, avg = pl.pallas_call(
        finish,
        out_shape=(
            jax.ShapeDtypeStruct((1, half), f32),
            jax.ShapeDtypeStruct((cls_dev, FLAT), f32),
        ),
        in_specs=[vmem],
        out_specs=(vmem, vmem),
        compiler_params=pltpu.CompilerParams(vmem_limit_bytes=2 * 1024 * 1024),
    )(out)
    return logev.reshape(half), avg


def solution(mesh):
    return jax.shard_map(
        local,
        mesh=mesh,
        in_specs=(
            P("loop", None),
            P(("loop", "grp"), None),
            P(("loop", "grp")),
            P(("loop", "grp")),
            P(("loop", "grp")),
        ),
        out_specs=(P(("loop", "grp")), P(("loop", "grp"), None)),
        check_vma=False,
    )
```
